512 devices in a mesh: blk: 32 (over x, z), uly: 4 (over y_lo, core), rep: 4 (over y_hi).
Axes of the slice: x: 4, y: 8 (y_hi: 4, y_lo: 2; y = y_hi * 2 + y_lo), z: 8, core: 2. Of those that a mesh axis runs over, the one named last changes fastest.
Arguments:
- queries: bfloat16 [65536, 1536], P(('rep', 'blk', 'uly')), parts along dimension 0, may hold values from -13 to 13
- key_input: bfloat16 [65536, 1536], P(('rep', 'blk', 'uly')), parts along dimension 0, may hold values from -5 to 5
- value_input: bfloat16 [65536, 1536], P(('rep', 'blk', 'uly')), parts along dimension 0, may hold values from -6 to 6
- grad_out: bfloat16 [65536, 1536], P(('rep', 'blk', 'uly')), parts along dimension 0, may hold values from -6 to 6
- keep_index: int32 [8192], P(('rep', 'blk', 'uly')), parts along dimension 0, may hold values from 0 to 16383, as said below
Outputs:
- grad_q: bfloat16 [65536, 1536], P(('rep', 'blk', 'uly')), parts along dimension 0
- grad_k: bfloat16 [65536, 1536], P(('rep', 'blk', 'uly')), parts along dimension 0
- grad_v: bfloat16 [65536, 1536], P(('rep', 'blk', 'uly')), parts along dimension 0
The draws below stay inside these ranges and needn't reach their ends.
There are 4 independent parts, one for each index of `rep`. The reference program is written for one: setup_inputs(seed, part) draws one part's arguments, and reference() takes and returns one part's arrays. A program takes and returns all parts, laid end to end along the dimension named above; each array names one. Nothing has to cross between parts.
Inputs may be any that keep to these rules, and one draw needn't show every extreme that they name: keep_index[j] lies in its cell, 8 * j to 8 * j + 7; the first and the last cell keep their outermost token.
All inputs are finite; a program needn't handle non-finite values.
Results may differ from the reference program's by a relative error of at most 0.035.
Values may be sent and summed in bfloat16 or wider, within the bound.
A program may use at most 64 MiB of HBM per device.

```python
import math
import jax
import jax.numpy as jnp
from jax import lax

HEADS = 12
HEAD_DIM = 128
CELL = 8
TOKENS = 16384
KEYS = 2048


def anchor_plan(key):
    base = jax.random.fold_in(key, 101)
    offsets = jax.random.randint(jax.random.fold_in(base, 1), (KEYS,), 0, CELL, dtype=jnp.int32)
    keep_index = jnp.arange(KEYS, dtype=jnp.int32) * CELL + offsets
    keep_index = keep_index.at[0].set(0).at[KEYS - 1].set(TOKENS - 1)
    return keep_index


def base_field(key, scale_low, scale_high):
    row_scale = jnp.exp(jax.random.uniform(jax.random.fold_in(key, 11), (TOKENS, 1), jnp.float32, math.log(scale_low), math.log(scale_high)))
    noise = jax.random.truncated_normal(jax.random.fold_in(key, 12), -4.0, 4.0, (TOKENS, HEADS * HEAD_DIM), jnp.float32)
    return noise * row_scale


def draw_keep_index(key, part):
    return anchor_plan(key)


def draw_queries(key, part):
    field = base_field(jax.random.fold_in(key, 21), 0.5, 2.0)
    return field.astype(jnp.bfloat16)


def draw_key_input(key, part):
    field = base_field(jax.random.fold_in(key, 31), 0.25, 1.0)
    return field.astype(jnp.bfloat16)


def shard_levels(key, shape, pieces, low, largest):
    level = 1.0
    for axis_at, parts in pieces:
        steps = jax.random.uniform(jax.random.fold_in(jax.random.fold_in(key, 6), axis_at), (parts,), jnp.float32, low / len(pieces), largest / len(pieces))
        level = level * jnp.repeat(jnp.exp(steps), shape[axis_at] // parts).reshape((-1,) + (1,) * (len(shape) - 1 - axis_at))
    return level


def normal_values(rng, shape, spread, limit, cuts=(), kind=jnp.bfloat16):
    array = spread * jax.random.normal(rng, shape, jnp.float32)
    if cuts:
        array = array * shard_levels(rng, shape, cuts, -0.22, 0.18)
    return jnp.clip(array, -limit, limit).astype(kind)


def setup_inputs(seed: int = 0, part: int = 0) -> dict:
    splits = jax.random.split(jax.random.key(seed), 6)
    part_keys = jax.random.split(jax.random.fold_in(splits[5], part), 6)
    return {
        "queries": draw_queries(jax.random.fold_in(jax.random.fold_in(splits[5], part), 71), part),
        "key_input": draw_key_input(jax.random.fold_in(jax.random.fold_in(splits[5], part), 71), part),
        "value_input": normal_values(part_keys[2], (TOKENS, HEADS * HEAD_DIM), 1.0, 6.0, ((0, 128),)),
        "grad_out": normal_values(part_keys[3], (TOKENS, HEADS * HEAD_DIM), 1.0, 6.0, ((0, 128),)),
        "keep_index": draw_keep_index(jax.random.fold_in(jax.random.fold_in(splits[5], part), 71), part),
    }


def reference(queries, key_input, value_input, grad_out, keep_index):
    score_scale = HEAD_DIM ** -0.5
    key_rows = jnp.take(key_input, keep_index, axis=0)
    value_rows = jnp.take(value_input, keep_index, axis=0)

    def heads_first(rows):
        return rows.reshape(rows.shape[0], HEADS, HEAD_DIM).transpose(1, 0, 2)

    def one_head(group):
        query_head, key_head, value_head, grad_head = group
        scores = jnp.dot(query_head, key_head.T, preferred_element_type=jnp.float32) * score_scale
        row_top = jnp.max(scores, axis=1, keepdims=True)
        log_total = row_top + jnp.log(jnp.sum(jnp.exp(scores - row_top), axis=1, keepdims=True))
        probs = jnp.exp(scores - log_total)
        weights = probs.astype(jnp.bfloat16)
        attended = jnp.dot(weights, value_head, preferred_element_type=jnp.float32).astype(jnp.bfloat16)
        row_delta = jnp.sum(attended.astype(jnp.float32) * grad_head.astype(jnp.float32), axis=1, keepdims=True)
        dprobs = jnp.dot(grad_head, value_head.T, preferred_element_type=jnp.float32)
        dscores = (probs * (dprobs - row_delta)).astype(jnp.bfloat16)
        query_grad = (jnp.dot(dscores, key_head, preferred_element_type=jnp.float32) * score_scale).astype(jnp.bfloat16)
        key_grad = (jnp.dot(dscores.T, query_head, preferred_element_type=jnp.float32) * score_scale).astype(jnp.bfloat16)
        value_grad = jnp.dot(weights.T, grad_head, preferred_element_type=jnp.float32).astype(jnp.bfloat16)
        return query_grad, key_grad, value_grad

    query_grads, key_grads, value_grads = lax.map(
        one_head, (heads_first(queries), heads_first(key_rows), heads_first(value_rows), heads_first(grad_out)))

    def rows_first(stack):
        return stack.transpose(1, 0, 2).reshape(stack.shape[1], HEADS * HEAD_DIM)

    blank = jnp.zeros((TOKENS, HEADS * HEAD_DIM), jnp.bfloat16)
    grad_k = blank.at[keep_index].set(rows_first(key_grads))
    grad_v = blank.at[keep_index].set(rows_first(value_grads))
    return rows_first(query_grads), grad_k, grad_v
```

```python
import functools

import jax
import jax.numpy as jnp
from jax import lax
from jax.experimental import pallas as pl
from jax.experimental.pallas import tpu as pltpu
from jax.sharding import PartitionSpec as P

HEAD_DIM = 128
CELL = 8
SCALE = HEAD_DIM ** -0.5
LOG2E = 1.4426950408889634
F32 = jnp.float32
BF16 = jnp.bfloat16
ULY = 4


def dot_nn(a, b):
    return lax.dot_general(a, b, (((1,), (0,)), ((), ())), preferred_element_type=F32)


def dot_nt(a, b):
    return lax.dot_general(a, b, (((1,), (1,)), ((), ())), preferred_element_type=F32)


def dot_tn(a, b):
    return lax.dot_general(a, b, (((0,), (0,)), ((), ())), preferred_element_type=F32)


def kernel(
    nx, nz, heads, tok, rows,
    idx_ref, k_ref, v_ref, q_ref, g_ref,
    dq_out, dk_out, dv_out,
    kvsend, kv, qb, gb, e_buf, dp_buf, m_buf, stats, stats_in, fin,
    dq_acc, dqb, dqr, dqs, part, rbuf, ybuf, gkv_send, gkv,
    loc_sem, xkv_s, xkv_r, xq_s, xq_r, xg_s, xg_r, y_s, y_r,
    ring_s, ring_r, sib_s, sib_r, red_s, red_r, yr_s, yr_r, xo_s, xo_r, xd_s, xd_r,
):
    width = heads * HEAD_DIM
    half = nz // 2
    nq = 2 * nx * tok
    tq = min(256, nq)
    blk = lax.axis_index("blk")
    uly = lax.axis_index("uly")
    x = blk // nz
    z = blk % nz
    y = uly // 2
    c = uly % 2
    right = {"blk": x * nz + (z + 1) % nz}
    left = {"blk": x * nz + (z + nz - 1) % nz}
    ypeer = {"uly": (1 - y) * 2 + c}
    sib = {"uly": y * 2 + (1 - c)}

    def xpeer(j):
        return {"blk": ((x + j) % nx) * nz + z}

    def send(src, dst, s_sem, r_sem, dev):
        return pltpu.make_async_remote_copy(
            src_ref=src, dst_ref=dst, send_sem=s_sem, recv_sem=r_sem,
            device_id=dev, device_id_type=pl.DeviceIdType.MESH)

    barrier = pltpu.get_barrier_semaphore()
    others = [xpeer(j) for j in range(1, nx)] + [right, left, ypeer, sib]
    for dev in others:
        pl.semaphore_signal(barrier, inc=1, device_id=dev, device_id_type=pl.DeviceIdType.MESH)

    hot = (lax.broadcasted_iota(jnp.int32, (tok, rows), 0)
           == lax.rem(idx_ref[...], tok)).astype(F32).astype(BF16)
    for a, ref in enumerate((k_ref, v_ref)):
        for g in range(nx):
            for h in range(heads):
                col = (g * heads + h) * HEAD_DIM
                kvsend[g, h, a] = dot_tn(hot, ref[:, col:col + HEAD_DIM]).astype(BF16)

    pl.semaphore_wait(barrier, len(others))

    xrow = pl.ds(pl.multiple_of(x * rows, rows), rows)
    own_rows = pl.ds(pl.multiple_of((c * nx + x) * tok, tok), tok)
    own_cols = pl.ds(pl.multiple_of(x * width, width), width)
    kv_x = []
    for j in range(1, nx):
        g = (x + j) % nx
        kv_x.append(send(kvsend.at[g], kv.at[:, :, 0, y, xrow], xkv_s.at[j - 1], xkv_r.at[j - 1], xpeer(j)))
        kv_x[-1].start()
    q_x = []
    for j in range(1, nx):
        cols = pl.ds(pl.multiple_of(((x + j) % nx) * width, width), width)
        for src, dst, ss, rs in ((q_ref, qb, xq_s, xq_r), (g_ref, gb, xg_s, xg_r)):
            q_x.append(send(src.at[:, cols], dst.at[own_rows], ss.at[j - 1], rs.at[j - 1], xpeer(j)))
            q_x[-1].start()
    kv_own = pltpu.make_async_copy(kvsend.at[x], kv.at[:, :, 0, y, xrow], loc_sem.at[0])
    kv_own.start()
    q_own = pltpu.make_async_copy(q_ref.at[:, own_cols], qb.at[own_rows], loc_sem.at[1])
    q_own.start()
    g_own = pltpu.make_async_copy(g_ref.at[:, own_cols], gb.at[own_rows], loc_sem.at[2])
    g_own.start()

    stats[...] = jnp.zeros_like(stats)
    for h in range(heads):
        stats[h, 0:1] = jnp.full((1, nq), -1e30, F32)
    dq_acc[...] = jnp.zeros_like(dq_acc)

    kv_own.wait()
    for copy in kv_x:
        copy.wait_recv()
    kv_y = send(kv.at[:, :, 0, y], kv.at[:, :, 0, y], y_s, y_r, ypeer)
    kv_y.start()
    kv_y.wait_recv()

    def ring_full(s):
        last = 0 if isinstance(s, int) and s == 1 else 2 * (s - 1)
        src_a = last
        src_b = 0 if isinstance(s, int) and s == 1 else last + 1
        return (send(kv.at[:, :, src_a], kv.at[:, :, 2 * s], ring_s.at[0, s - 1], ring_r.at[0, s - 1], right),
                send(kv.at[:, :, src_b], kv.at[:, :, 2 * s + 1], ring_s.at[1, s - 1], ring_r.at[1, s - 1], left))

    def ring_half():
        last = 2 * (half - 1)
        return (send(kv.at[:, 0, last], kv.at[:, 0, 1], ring_s.at[0, half - 1], ring_r.at[0, half - 1], right),
                send(kv.at[:, 1, last + 1], kv.at[:, 1, 1], ring_s.at[1, half - 1], ring_r.at[1, half - 1], left))

    def forward(s):
        @pl.when(s < half - 1)
        def _():
            for copy in ring_full(s + 1):
                copy.start()

        @pl.when(s == half - 1)
        def _():
            for copy in ring_half():
                copy.start()

    for copy in ring_full(1):
        copy.start()

    q_own.wait()
    g_own.wait()
    for copy in q_x:
        copy.wait_recv()
    mine = pl.ds(pl.multiple_of(c * nx * tok, tok), nx * tok)
    share = [send(qb.at[mine], qb.at[mine], sib_s.at[0], sib_r.at[0], sib),
             send(gb.at[mine], gb.at[mine], sib_s.at[1], sib_r.at[1], sib)]
    for copy in share:
        copy.start()
    for copy in ring_full(1):
        copy.wait_recv()
    forward(jnp.int32(1))
    for copy in share:
        copy.wait_recv()

    def pass1(s):
        def head(h, carry):
            lanes = pl.ds(pl.multiple_of(h * HEAD_DIM, HEAD_DIM), HEAD_DIM)
            keys = kv[h, 0, pl.ds(2 * s, 2)].reshape(4 * nx * rows, HEAD_DIM)
            vals = kv[h, 1, pl.ds(2 * s, 2)].reshape(4 * nx * rows, HEAD_DIM)
            for t in range(nq // tq):
                ts = slice(t * tq, (t + 1) * tq)
                sc = dot_nt(keys, qb[ts, lanes]) * (SCALE * LOG2E)
                dp = dot_nt(vals, gb[ts, lanes])
                m_old = stats[h, 0:1, ts]
                m_new = jnp.maximum(m_old, jnp.max(sc, axis=0, keepdims=True))
                e = jnp.exp2(sc - m_new)
                a = jnp.exp2(m_old - m_new)
                e_buf[s, h, :, ts] = e
                dp_buf[s, h, :, ts] = dp
                m_buf[s, h, 0:1, ts] = m_new
                stats[h, 0:1, ts] = m_new
                stats[h, 1:2, ts] = stats[h, 1:2, ts] * a + jnp.sum(e, axis=0, keepdims=True)
                stats[h, 2:3, ts] = stats[h, 2:3, ts] * a + jnp.sum(e * dp, axis=0, keepdims=True)
            return carry
        lax.fori_loop(0, heads, head, 0)

    def gather_step(s, carry):
        pass1(s)

        @pl.when(s < half - 1)
        def _():
            for copy in ring_full(s + 1):
                copy.wait_recv()
            forward(s + 1)
        return carry

    lax.fori_loop(1, half, gather_step, 0)
    for copy in ring_half():
        copy.wait_recv()
    pass1(0)

    join = send(stats, stats_in, sib_s.at[2], sib_r.at[2], sib)
    join.start()
    join.wait()
    for h in range(heads):
        m1, m2 = stats[h, 0:1], stats_in[h, 0:1]
        m = jnp.maximum(m1, m2)
        a1, a2 = jnp.exp2(m1 - m), jnp.exp2(m2 - m)
        inv = 1.0 / (stats[h, 1:2] * a1 + stats_in[h, 1:2] * a2)
        fin[h, 0:1] = m
        fin[h, 1:2] = inv
        fin[h, 2:3] = (stats[h, 2:3] * a1 + stats_in[h, 2:3] * a2) * inv

    def pass2(s):
        def head(h, carry):
            lanes = pl.ds(pl.multiple_of(h * HEAD_DIM, HEAD_DIM), HEAD_DIM)
            keys = kv[h, 0, pl.ds(2 * s, 2)].reshape(4 * nx * rows, HEAD_DIM)
            dk = jnp.zeros((4 * nx * rows, HEAD_DIM), F32)
            dv = jnp.zeros((4 * nx * rows, HEAD_DIM), F32)
            for t in range(nq // tq):
                ts = slice(t * tq, (t + 1) * tq)
                r = jnp.exp2(m_buf[s, h, 0:1, ts] - fin[h, 0:1, ts]) * fin[h, 1:2, ts]
                p = e_buf[s, h, :, ts] * r
                ds = (p * (dp_buf[s, h, :, ts] - fin[h, 2:3, ts])).astype(BF16)
                dv = dv + dot_nn(p.astype(BF16), gb[ts, lanes])
                dk = dk + dot_nn(ds, qb[ts, lanes])
                dq_acc[h, :, ts] = dq_acc[h, :, ts] + dot_tn(keys, ds)
            part[h, 0, pl.ds(2 * s, 2)] = dk.astype(BF16).reshape(2, 2, nx * rows, HEAD_DIM)
            part[h, 1, pl.ds(2 * s, 2)] = dv.astype(BF16).reshape(2, 2, nx * rows, HEAD_DIM)
            return carry
        lax.fori_loop(0, heads, head, 0)

    def reduce_first():
        return (send(part.at[:, 0, 1], rbuf.at[0, 0, :, 0], red_s.at[0, 0], red_r.at[0, 0], right),
                send(part.at[:, 1, 1], rbuf.at[1, 0, :, 1], red_s.at[1, 0], red_r.at[1, 0], left))

    def reduce_full(t):
        d = half - t
        return (send(part.at[:, :, 2 * d + 1], rbuf.at[0, t], red_s.at[0, t], red_r.at[0, t], right),
                send(part.at[:, :, 2 * d], rbuf.at[1, t], red_s.at[1, t], red_r.at[1, t], left))

    def add_in(t, d, a):
        part[:, a, 2 * d + 1] = (part[:, a, 2 * d + 1].astype(F32) + rbuf[0, t, :, a].astype(F32)).astype(BF16)

    def add_in_left(t, d, a):
        part[:, a, 2 * d] = (part[:, a, 2 * d].astype(F32) + rbuf[1, t, :, a].astype(F32)).astype(BF16)

    def reduce_step(t, carry):
        d = half - t
        pass2(lax.rem(d, half))

        @pl.when(t == 0)
        def _():
            for copy in reduce_first():
                copy.start()

        @pl.when(t == 1)
        def _():
            for copy in reduce_first():
                copy.wait_recv()
            add_in(0, d, 0)
            add_in_left(0, d, 1)

        @pl.when(t > 1)
        def _():
            for copy in reduce_full(t - 1):
                copy.wait_recv()
            for a in range(2):
                add_in(t - 1, d, a)
                add_in_left(t - 1, d, a)

        @pl.when(t > 0)
        def _():
            for copy in reduce_full(t):
                copy.start()
        return carry

    lax.fori_loop(0, half, reduce_step, 0)

    for h in range(heads):
        for cc in range(2):
            for xs in range(nx):
                at = (cc * nx + xs) * tok
                dqb[cc, xs, :, h * HEAD_DIM:(h + 1) * HEAD_DIM] = (
                    jnp.transpose(dq_acc[h, :, at:at + tok]) * SCALE).astype(BF16)
    dq_sib = send(dqb.at[1 - c], dqr, sib_s.at[3], sib_r.at[3], sib)
    dq_sib.start()
    dq_sib.wait()
    for xs in range(nx):
        dqs[xs] = (dqb[c, xs].astype(F32) + dqr[xs].astype(F32)).astype(BF16)
    dq_x = []
    for j in range(1, nx):
        dq_x.append(send(dqs.at[(x + j) % nx], dq_out.at[:, own_cols], xd_s.at[j - 1], xd_r.at[j - 1], xpeer(j)))
        dq_x[-1].start()
    dq_own = pltpu.make_async_copy(dqs.at[x], dq_out.at[:, own_cols], loc_sem.at[3])
    dq_own.start()

    for copy in reduce_full(half - 1):
        copy.wait_recv()
    for h in range(heads):
        for a in range(2):
            total = (part[h, a, 0].astype(F32) + rbuf[0, half - 1, h, a].astype(F32)
                     + rbuf[1, half - 1, h, a].astype(F32))
            part[h, a, 0] = total.astype(BF16)
    yr = send(part.at[:, :, 0, 1 - y], ybuf, yr_s, yr_r, ypeer)
    yr.start()
    yr.wait()
    for h in range(heads):
        for a in range(2):
            total = part[h, a, 0, y].astype(F32) + ybuf[h, a].astype(F32)
            if a == 0:
                total = total * SCALE
            total = total.astype(BF16)
            for xs in range(nx):
                gkv_send[xs, h, a] = total[xs * rows:(xs + 1) * rows]
    out_x = []
    for j in range(1, nx):
        out_x.append(send(gkv_send.at[(x + j) % nx], gkv.at[x], xo_s.at[j - 1], xo_r.at[j - 1], xpeer(j)))
        out_x[-1].start()
    out_own = pltpu.make_async_copy(gkv_send.at[x], gkv.at[x], loc_sem.at[4])
    out_own.start()
    out_own.wait()
    for copy in out_x:
        copy.wait_recv()
    for a, ref in enumerate((dk_out, dv_out)):
        for g in range(nx):
            for h in range(heads):
                col = (g * heads + h) * HEAD_DIM
                ref[:, col:col + HEAD_DIM] = dot_nn(hot, gkv[g, h, a]).astype(BF16)

    for copy in kv_x + q_x + [kv_y] + share:
        copy.wait_send()
    dq_own.wait()
    for copy in dq_x:
        copy.wait()
    for copy in out_x:
        copy.wait_send()

    def drain(s, carry):
        for copy in ring_full(s):
            copy.wait_send()
        for copy in reduce_full(s):
            copy.wait_send()
        return carry

    lax.fori_loop(1, half, drain, 0)
    for copy in ring_half() + reduce_first():
        copy.wait_send()


def per_device(nx, nz, queries, key_input, value_input, grad_out, keep_index):
    tok, columns = queries.shape
    rows = keep_index.shape[0]
    heads = columns // HEAD_DIM // nx
    width = heads * HEAD_DIM
    half = nz // 2
    nq = 2 * nx * tok
    nk = 4 * nx * rows
    slab = (nx * rows, HEAD_DIM)
    dma = pltpu.SemaphoreType.DMA
    vmem = pltpu.VMEM
    out = jax.ShapeDtypeStruct((tok, columns), BF16)
    in_vmem = pl.BlockSpec(memory_space=pltpu.VMEM)
    in_any = pl.BlockSpec(memory_space=pl.ANY)
    flops = 2 * 6 * heads * nq * (half * nk) * HEAD_DIM
    return pl.pallas_call(
        functools.partial(kernel, nx, nz, heads, tok, rows),
        out_shape=(out, out, out),
        in_specs=[in_vmem, in_vmem, in_vmem, in_any, in_any],
        out_specs=(in_vmem, in_vmem, in_vmem),
        scratch_shapes=[
            vmem((nx, heads, 2, rows, HEAD_DIM), BF16),
            vmem((heads, 2, nz, 2) + slab, BF16),
            vmem((nq, width), BF16),
            vmem((nq, width), BF16),
            vmem((half, heads, nk, nq), F32),
            vmem((half, heads, nk, nq), F32),
            vmem((half, heads, 8, nq), F32),
            vmem((heads, 8, nq), F32),
            vmem((heads, 8, nq), F32),
            vmem((heads, 8, nq), F32),
            vmem((heads, HEAD_DIM, nq), F32),
            vmem((2, nx, tok, width), BF16),
            vmem((nx, tok, width), BF16),
            vmem((nx, tok, width), BF16),
            vmem((heads, 2, nz, 2) + slab, BF16),
            vmem((2, half, heads, 2, 2) + slab, BF16),
            vmem((heads, 2) + slab, BF16),
            vmem((nx, heads, 2, rows, HEAD_DIM), BF16),
            vmem((nx, heads, 2, rows, HEAD_DIM), BF16),
            dma((5,)),
            dma((nx - 1,)), dma((nx - 1,)),
            dma((nx - 1,)), dma((nx - 1,)),
            dma((nx - 1,)), dma((nx - 1,)),
            dma, dma,
            dma((2, half)), dma((2, half)),
            dma((4,)), dma((4,)),
            dma((2, half)), dma((2, half)),
            dma, dma,
            dma((nx - 1,)), dma((nx - 1,)),
            dma((nx - 1,)), dma((nx - 1,)),
        ],
        compiler_params=pltpu.CompilerParams(
            collective_id=0, has_side_effects=True, vmem_limit_bytes=56 * 2 ** 20),
        cost_estimate=pl.CostEstimate(
            flops=flops, bytes_accessed=7 * tok * columns * 2, transcendentals=heads * nq * half * nk),
    )(keep_index.reshape(1, rows), key_input, value_input, queries, grad_out)


def build(mesh, nx, nz):
    rows_spec = P(("rep", "blk", "uly"), None)
    return jax.shard_map(
        functools.partial(per_device, nx, nz), mesh=mesh,
        in_specs=(rows_spec,) * 4 + (P(("rep", "blk", "uly")),),
        out_specs=(rows_spec,) * 3, check_vma=False)


def solution(mesh):
    return build(mesh, 4, 8)
```

```python
import functools

import jax
import jax.numpy as jnp
from jax import lax
from jax.experimental import pallas as pl
from jax.experimental.pallas import tpu as pltpu
from jax.sharding import PartitionSpec as P

HEAD_DIM = 128
CELL = 8
SCALE = HEAD_DIM ** -0.5
LOG2E = 1.4426950408889634
F32 = jnp.float32
BF16 = jnp.bfloat16
ULY = 4


def dot_nn(a, b):
    return lax.dot_general(a, b, (((1,), (0,)), ((), ())), preferred_element_type=F32)


def dot_nt(a, b):
    return lax.dot_general(a, b, (((1,), (1,)), ((), ())), preferred_element_type=F32)


def dot_tn(a, b):
    return lax.dot_general(a, b, (((0,), (0,)), ((), ())), preferred_element_type=F32)


def one_hot(idx_ref, tok, rows):
    return (lax.broadcasted_iota(jnp.int32, (tok, rows), 0)
            == lax.rem(idx_ref[...], tok)).astype(F32).astype(BF16)


def kernel(
    nx, nz, heads, tok, rows,
    idx_ref, k_ref, v_ref, q_ref, g_ref,
    dq_out, gkv,
    kvsend, kv, qb, gb, e_buf, dp_buf, m_buf, stats, stats_in, fin,
    dq_acc, dqb, dqr, dqs, part, rs_buf, rr_buf, ys_buf, yr_buf, gkv_send,
    loc_sem, xkv_s, xkv_r, xq_s, xq_r, xg_s, xg_r, y_s, y_r,
    ring_s, ring_r, sib_s, sib_r, join_s, join_r, red_s, red_r, yr_s, yr_r, xo_s, xo_r, xd_s, xd_r,
):
    width = heads * HEAD_DIM
    half = nz // 2
    hq = nx * tok
    nq = 2 * hq
    nk = 4 * nx * rows
    tq = min(256, hq)
    blk = lax.axis_index("blk")
    uly = lax.axis_index("uly")
    x = blk // nz
    z = blk % nz
    y = uly // 2
    c = uly % 2
    right = {"blk": x * nz + (z + 1) % nz}
    left = {"blk": x * nz + (z + nz - 1) % nz}
    ypeer = {"uly": (1 - y) * 2 + c}
    sib = {"uly": y * 2 + (1 - c)}
    hop = [1, nx - 1] + list(range(2, nx - 1)) if nx > 2 else [1]

    def xpeer(j):
        return {"blk": ((x + j) % nx) * nz + z}

    def send(src, dst, s_sem, r_sem, dev):
        return pltpu.make_async_remote_copy(
            src_ref=src, dst_ref=dst, send_sem=s_sem, recv_sem=r_sem,
            device_id=dev, device_id_type=pl.DeviceIdType.MESH)

    def start(copies):
        for copy in copies:
            copy.start()

    def received(copies):
        for copy in copies:
            copy.wait_recv()

    def sent(copies):
        for copy in copies:
            copy.wait_send()

    barrier = pltpu.get_barrier_semaphore()
    others = [xpeer(j) for j in hop] + [right, left, ypeer, sib]
    for dev in others:
        pl.semaphore_signal(barrier, inc=1, device_id=dev, device_id_type=pl.DeviceIdType.MESH)

    hot = one_hot(idx_ref, tok, rows)
    for a, ref in enumerate((k_ref, v_ref)):
        for g in range(nx):
            for h in range(heads):
                col = (g * heads + h) * HEAD_DIM
                kvsend[g, h, a] = dot_tn(hot, ref[:, col:col + HEAD_DIM]).astype(BF16)

    pl.semaphore_wait(barrier, len(others))

    xrow = pl.ds(pl.multiple_of(x * rows, rows), rows)

    def token_rows(j):
        return pl.ds(pl.multiple_of((c * nx + (x + nx - j) % nx) * tok, tok), tok)

    def group_cols(j):
        return pl.ds(pl.multiple_of(((x + j) % nx) * width, width), width)

    kv_x = [send(kvsend.at[(x + j) % nx], kv.at[:, :, 0, y, xrow], xkv_s.at[j - 1], xkv_r.at[j - 1], xpeer(j))
            for j in hop]
    start(kv_x)
    kv_own = pltpu.make_async_copy(kvsend.at[x], kv.at[:, :, 0, y, xrow], loc_sem.at[0])
    kv_own.start()
    q_x = {j: [send(q_ref.at[:, group_cols(j)], qb.at[token_rows(0)], xq_s.at[j - 1], xq_r.at[j - 1], xpeer(j)),
               send(g_ref.at[:, group_cols(j)], gb.at[token_rows(0)], xg_s.at[j - 1], xg_r.at[j - 1], xpeer(j))]
           for j in hop}
    for j in hop:
        start(q_x[j])
    q_own = [pltpu.make_async_copy(q_ref.at[:, group_cols(0)], qb.at[token_rows(0)], loc_sem.at[1]),
             pltpu.make_async_copy(g_ref.at[:, group_cols(0)], gb.at[token_rows(0)], loc_sem.at[2])]
    start(q_own)

    share = {0: [send(q_ref.at[:, group_cols(0)], qb.at[token_rows(0)], sib_s.at[0, 0], sib_r.at[0, 0], sib),
                 send(g_ref.at[:, group_cols(0)], gb.at[token_rows(0)], sib_s.at[1, 0], sib_r.at[1, 0], sib)]}
    for j in hop:
        share[j] = [send(qb.at[token_rows(j)], qb.at[token_rows(j)], sib_s.at[0, j], sib_r.at[0, j], sib),
                    send(gb.at[token_rows(j)], gb.at[token_rows(j)], sib_s.at[1, j], sib_r.at[1, j], sib)]
    start(share[0])

    stats[...] = jnp.zeros_like(stats)
    for h in range(heads):
        stats[h, 0:1] = jnp.full((1, nq), -1e30, F32)
    dq_acc[...] = jnp.zeros_like(dq_acc)

    def ring(kind, s):
        def cut(slot, a):
            if kind == 0:
                return kv.at[1:heads, a, slot, y]
            return kv.at[0, a, slot]
        a_src, b_src = (0, 0) if s == 1 else (2 * s - 2, 2 * s - 1)
        if s < half:
            ways = ((a_src, 2 * s, slice(None)), (b_src, 2 * s + 1, slice(None)))
        else:
            ways = ((a_src, 1, 0), (b_src, 1, 1))
        return [send(cut(src, a), cut(dst, a), ring_s.at[kind, w, s - 1], ring_r.at[kind, w, s - 1], dev)
                for w, ((src, dst, a), dev) in enumerate(zip(ways, (right, left)))]

    def over_y(slot):
        return send(kv.at[1:heads, :, slot, y], kv.at[1:heads, :, slot, y], y_s.at[slot], y_r.at[slot], ypeer)

    def handle(s):
        slots = (2 * s, 2 * s + 1) if s < half else (1,)
        for kind in range(2):
            received(ring(kind, s))
            if s < half:
                start(ring(kind, s + 1))
            if kind == 0:
                start([over_y(slot) for slot in slots])

    kv_own.wait()
    received(kv_x)
    start(ring(0, 1))
    y_first = send(kv.at[0, :, 0, y], kv.at[0, :, 0, y], y_s.at[nz], y_r.at[nz], ypeer)
    start([y_first, over_y(0)])
    received([y_first])
    start(ring(1, 1))
    for copy in q_own:
        copy.wait()
    early = min(2, half)
    handle(1)
    for j in hop:
        received(q_x[j])
        start(share[j])
    for s in range(2, early + 1):
        handle(s)

    def pass1(s, qh, h):
        lanes = pl.ds(pl.multiple_of(h * HEAD_DIM, HEAD_DIM), HEAD_DIM)
        keys = kv[h, 0, pl.ds(2 * s, 2)].reshape(nk, HEAD_DIM)
        vals = kv[h, 1, pl.ds(2 * s, 2)].reshape(nk, HEAD_DIM)
        for t in range(hq // tq):
            ts = pl.ds(pl.multiple_of(qh * hq + t * tq, tq), tq)
            sc = dot_nt(keys, qb[ts, lanes]) * (SCALE * LOG2E)
            dp = dot_nt(vals, gb[ts, lanes])
            m_old = stats[h, 0:1, ts]
            m_new = jnp.maximum(m_old, jnp.max(sc, axis=0, keepdims=True))
            e = jnp.exp2(sc - m_new)
            a = jnp.exp2(m_old - m_new)
            e_buf[s, h, :, ts] = e
            dp_buf[s, h, :, ts] = dp
            m_buf[s, h, 0:1, ts] = m_new
            stats[h, 0:1, ts] = m_new
            stats[h, 1:2, ts] = stats[h, 1:2, ts] * a + jnp.sum(e, axis=0, keepdims=True)
            stats[h, 2:3, ts] = stats[h, 2:3, ts] * a + jnp.sum(e * dp, axis=0, keepdims=True)

    def gather_step(i, carry):
        n = i // 2
        s = n + 1
        later = lax.rem(i, 2)
        for m in range(half - 1):
            @pl.when(i == 2 * m)
            def _():
                if m >= 1 and m + 2 <= half:
                    handle(m + 2)
                received([over_y(2 * m + 2), over_y(2 * m + 3)])

        @pl.when(i == 1)
        def _():
            for j in [0] + hop:
                received(share[j])

        def head(h, inner):
            pass1(s, lax.rem(c + later, 2), h)
            return inner
        lax.fori_loop(0, heads, head, 0)
        return carry

    lax.fori_loop(0, 2 * (half - 1), gather_step, 0)
    received([over_y(0), over_y(1)])

    def join(h):
        return send(stats.at[h], stats_in.at[h], join_s.at[h], join_r.at[h], sib)

    def last_head(h, carry):
        def both(qh, inner):
            pass1(0, qh, h)
            return inner
        lax.fori_loop(0, 2, both, 0)
        join(h).start()
        return carry

    lax.fori_loop(0, heads, last_head, 0)

    def finish_stats(h):
        join(h).wait_recv()
        m1, m2 = stats[h, 0:1], stats_in[h, 0:1]
        m = jnp.maximum(m1, m2)
        a1, a2 = jnp.exp2(m1 - m), jnp.exp2(m2 - m)
        inv = 1.0 / (stats[h, 1:2] * a1 + stats_in[h, 1:2] * a2)
        fin[h, 0:1] = m
        fin[h, 1:2] = inv
        fin[h, 2:3] = (stats[h, 2:3] * a1 + stats_in[h, 2:3] * a2) * inv

    def pass2(s, h):
        lanes = pl.ds(pl.multiple_of(h * HEAD_DIM, HEAD_DIM), HEAD_DIM)
        keys = kv[h, 0, pl.ds(2 * s, 2)].reshape(nk, HEAD_DIM)
        dk = jnp.zeros((nk, HEAD_DIM), F32)
        dv = jnp.zeros((nk, HEAD_DIM), F32)
        for t in range(nq // tq):
            ts = slice(t * tq, (t + 1) * tq)
            r = jnp.exp2(m_buf[s, h, 0:1, ts] - fin[h, 0:1, ts]) * fin[h, 1:2, ts]
            p = e_buf[s, h, :, ts] * r
            ds = (p * (dp_buf[s, h, :, ts] - fin[h, 2:3, ts])).astype(BF16)
            dv = dv + dot_nn(p.astype(BF16), gb[ts, lanes])
            dk = dk + dot_nn(ds, qb[ts, lanes])
            dq_acc[h, :, ts] = dq_acc[h, :, ts] + dot_tn(keys, ds)
        part[h, 0, pl.ds(2 * s, 2)] = dk.astype(BF16).reshape(2, 2, nx * rows, HEAD_DIM)
        part[h, 1, pl.ds(2 * s, 2)] = dv.astype(BF16).reshape(2, 2, nx * rows, HEAD_DIM)

    def mine(kind, slot, a):
        return part.at[1:heads, a, slot, y] if kind == 0 else part.at[0, a, slot]

    def box(kind, w, t, a):
        return rs_buf.at[w, t, :, a] if kind == 0 else rr_buf.at[w, t, a]

    def reduce_half(kind):
        return [send(mine(kind, 1, w), box(kind, w, 0, w), red_s.at[kind, w, 0], red_r.at[kind, w, 0], dev)
                for w, dev in enumerate((right, left))]

    def reduce_full(kind, t):
        d = half - t
        return [send(mine(kind, 2 * d + 1 - w, slice(None)), box(kind, w, t, slice(None)),
                     red_s.at[kind, w, t], red_r.at[kind, w, t], dev)
                for w, dev in enumerate((right, left))]

    def reduce_y(slot):
        return send(part.at[1:heads, :, slot, 1 - y], ys_buf.at[slot], yr_s.at[slot], yr_r.at[slot], ypeer)

    def add_y(slot):
        reduce_y(slot).wait_recv()
        part[1:heads, :, slot, y] = (part[1:heads, :, slot, y].astype(F32) + ys_buf[slot].astype(F32)).astype(BF16)

    def add_box(kind, w, t, slot, a):
        if kind == 0:
            part[1:heads, a, slot, y] = (
                part[1:heads, a, slot, y].astype(F32) + rs_buf[w, t, :, a].astype(F32)).astype(BF16)
        else:
            part[0, a, slot] = (part[0, a, slot].astype(F32) + rr_buf[w, t, a].astype(F32)).astype(BF16)

    def produce(t):
        s = lax.rem(half - t, half)

        def head(h, carry):
            @pl.when(t == 0)
            def _():
                finish_stats(h)
            pass2(s, h)

            @pl.when((t == 0) & (h == 0))
            def _():
                start(reduce_half(1))
            return carry
        lax.fori_loop(0, heads, head, 0)

        @pl.when(t == 0)
        def _():
            start([reduce_y(1), reduce_y(0)])

        @pl.when(t > 0)
        def _():
            start([reduce_y(2 * s + 1), reduce_y(2 * s)])

    def pass_on(t):
        d = half - t

        @pl.when(t == 0)
        def _():
            add_y(1)
            start(reduce_half(0))

        @pl.when(t > 0)
        def _():
            for kind in (1, 0):
                if kind == 0:
                    add_y(2 * d + 1)
                    add_y(2 * d)

                @pl.when(t == 1)
                def _():
                    received(reduce_half(kind))
                    for w in range(2):
                        add_box(kind, w, 0, 2 * d + 1 - w, w)

                @pl.when(t > 1)
                def _():
                    received(reduce_full(kind, t - 1))
                    for w in range(2):
                        for a in range(2):
                            add_box(kind, w, t - 1, 2 * d + 1 - w, a)
                start(reduce_full(kind, t))

    dq_sib = send(dqb.at[1 - c], dqr, sib_s.at[0, nx], sib_r.at[0, nx], sib)

    def reduce_step(t, carry):
        @pl.when(t < half)
        def _():
            produce(t)

        @pl.when(t == half)
        def _():
            for h in range(heads):
                for cc in range(2):
                    for xs in range(nx):
                        at = (cc * nx + xs) * tok
                        dqb[cc, xs, :, h * HEAD_DIM:(h + 1) * HEAD_DIM] = (
                            jnp.transpose(dq_acc[h, :, at:at + tok]) * SCALE).astype(BF16)
            dq_sib.start()

        @pl.when(t > 0)
        def _():
            pass_on(t - 1)
        return carry

    lax.fori_loop(0, half + 1, reduce_step, 0)

    dq_sib.wait()
    for xs in range(nx):
        dqs[xs] = (dqb[c, xs].astype(F32) + dqr[xs].astype(F32)).astype(BF16)
    dq_x = [send(dqs.at[(x + j) % nx], dq_out.at[:, group_cols(0)], xd_s.at[j - 1], xd_r.at[j - 1], xpeer(j))
            for j in hop]
    start(dq_x)
    dq_own = pltpu.make_async_copy(dqs.at[x], dq_out.at[:, group_cols(0)], loc_sem.at[3])
    dq_own.start()

    received(reduce_full(1, half - 1))
    part[0, :, 0] = (part[0, :, 0].astype(F32) + rr_buf[0, half - 1].astype(F32)
                     + rr_buf[1, half - 1].astype(F32)).astype(BF16)
    y_last = send(part.at[0, :, 0, 1 - y], yr_buf, yr_s.at[nz], yr_r.at[nz], ypeer)
    y_last.start()

    def put(h, a, total):
        if a == 0:
            total = total * SCALE
        total = total.astype(BF16)
        for xs in range(nx):
            gkv_send[xs, h, a] = total[xs * rows:(xs + 1) * rows]

    reduce_y(0).wait_recv()
    received(reduce_full(0, half - 1))
    for h in range(1, heads):
        for a in range(2):
            put(h, a, part[h, a, 0, y].astype(F32) + ys_buf[0, h - 1, a].astype(F32)
                + rs_buf[0, half - 1, h - 1, a].astype(F32) + rs_buf[1, half - 1, h - 1, a].astype(F32))
    y_last.wait_recv()
    for a in range(2):
        put(0, a, part[0, a, 0, y].astype(F32) + yr_buf[a].astype(F32))
    out_x = [send(gkv_send.at[(x + j) % nx], gkv.at[x], xo_s.at[j - 1], xo_r.at[j - 1], xpeer(j)) for j in hop]
    start(out_x)
    out_own = pltpu.make_async_copy(gkv_send.at[x], gkv.at[x], loc_sem.at[4])
    out_own.start()

    sent(kv_x)
    for j in hop:
        sent(q_x[j])
    for j in [0] + hop:
        sent(share[j])
    for kind in range(2):
        for s in range(1, half + 1):
            sent(ring(kind, s))
        sent(reduce_half(kind))
        for t in range(1, half):
            sent(reduce_full(kind, t))
    for slot in range(nz):
        sent([over_y(slot), reduce_y(slot)])
    sent([y_first, y_last])
    for h in range(heads):
        join(h).wait_send()
    dq_own.wait()
    for copy in dq_x:
        copy.wait()
    out_own.wait()
    for copy in out_x:
        copy.wait()


def place(nx, heads, tok, rows, idx_ref, dq_ref, gkv_ref, dq_out, dk_out, dv_out):
    dq_out[...] = dq_ref[...]
    hot = one_hot(idx_ref, tok, rows)
    for a, ref in enumerate((dk_out, dv_out)):
        for g in range(nx):
            for h in range(heads):
                col = (g * heads + h) * HEAD_DIM
                ref[:, col:col + HEAD_DIM] = dot_nn(hot, gkv_ref[g, h, a]).astype(BF16)


def per_device(nx, nz, queries, key_input, value_input, grad_out, keep_index):
    tok, columns = queries.shape
    rows = keep_index.shape[0]
    heads = columns // HEAD_DIM // nx
    width = heads * HEAD_DIM
    half = nz // 2
    nq = 2 * nx * tok
    nk = 4 * nx * rows
    slab = (nx * rows, HEAD_DIM)
    dma = pltpu.SemaphoreType.DMA
    vmem = pltpu.VMEM
    out = jax.ShapeDtypeStruct((tok, columns), BF16)
    compact = (nx, heads, 2, rows, HEAD_DIM)
    in_vmem = pl.BlockSpec(memory_space=pltpu.VMEM)
    in_any = pl.BlockSpec(memory_space=pl.ANY)
    flops = 2 * 6 * heads * nq * (half * nk) * HEAD_DIM
    index = keep_index.reshape(1, rows)
    dq, gkv = pl.pallas_call(
        functools.partial(kernel, nx, nz, heads, tok, rows),
        out_shape=(out, jax.ShapeDtypeStruct(compact, BF16)),
        in_specs=[in_vmem, in_vmem, in_vmem, in_any, in_any],
        out_specs=(in_vmem, in_vmem),
        scratch_shapes=[
            vmem(compact, BF16),
            vmem((heads, 2, nz, 2) + slab, BF16),
            vmem((nq, width), BF16),
            vmem((nq, width), BF16),
            vmem((half, heads, nk, nq), F32),
            vmem((half, heads, nk, nq), F32),
            vmem((half, heads, 8, nq), F32),
            vmem((heads, 8, nq), F32),
            vmem((heads, 8, nq), F32),
            vmem((heads, 8, nq), F32),
            vmem((heads, HEAD_DIM, nq), F32),
            vmem((2, nx, tok, width), BF16),
            vmem((nx, tok, width), BF16),
            vmem((nx, tok, width), BF16),
            vmem((heads, 2, nz, 2) + slab, BF16),
            vmem((2, half, heads - 1, 2) + slab, BF16),
            vmem((2, half, 2, 2) + slab, BF16),
            vmem((nz, heads - 1, 2) + slab, BF16),
            vmem((2,) + slab, BF16),
            vmem(compact, BF16),
            dma((5,)),
            dma((nx - 1,)), dma((nx - 1,)),
            dma((nx - 1,)), dma((nx - 1,)),
            dma((nx - 1,)), dma((nx - 1,)),
            dma((nz + 1,)), dma((nz + 1,)),
            dma((2, 2, half)), dma((2, 2, half)),
            dma((2, nx + 1)), dma((2, nx + 1)),
            dma((heads,)), dma((heads,)),
            dma((2, 2, half)), dma((2, 2, half)),
            dma((nz + 1,)), dma((nz + 1,)),
            dma((nx - 1,)), dma((nx - 1,)),
            dma((nx - 1,)), dma((nx - 1,)),
        ],
        compiler_params=pltpu.CompilerParams(
            collective_id=0, has_side_effects=True, vmem_limit_bytes=56 * 2 ** 20),
        cost_estimate=pl.CostEstimate(
            flops=flops, bytes_accessed=7 * tok * columns * 2, transcendentals=heads * nq * half * nk),
    )(index, key_input, value_input, queries, grad_out)
    return pl.pallas_call(
        functools.partial(place, nx, heads, tok, rows),
        out_shape=(out, out, out),
        in_specs=[in_vmem] * 3,
        out_specs=(in_vmem,) * 3,
    )(index, dq, gkv)


def build(mesh, nx, nz):
    rows_spec = P(("rep", "blk", "uly"), None)
    return jax.shard_map(
        functools.partial(per_device, nx, nz), mesh=mesh,
        in_specs=(rows_spec,) * 4 + (P(("rep", "blk", "uly")),),
        out_specs=(rows_spec,) * 3, check_vma=False)


def solution(mesh):
    return build(mesh, 4, 8)
```

```python
import functools

import jax
import jax.numpy as jnp
from jax import lax
from jax.experimental import pallas as pl
from jax.experimental.pallas import tpu as pltpu
from jax.sharding import PartitionSpec as P

HEAD_DIM = 128
CELL = 8
SCALE = HEAD_DIM ** -0.5
LOG2E = 1.4426950408889634
F32 = jnp.float32
BF16 = jnp.bfloat16
ULY = 4


def dot_nn(a, b):
    return lax.dot_general(a, b, (((1,), (0,)), ((), ())), preferred_element_type=F32)


def dot_nt(a, b):
    return lax.dot_general(a, b, (((1,), (1,)), ((), ())), preferred_element_type=F32)


def dot_tn(a, b):
    return lax.dot_general(a, b, (((0,), (0,)), ((), ())), preferred_element_type=F32)


def one_hot(idx_ref, tok, rows):
    return (lax.broadcasted_iota(jnp.int32, (tok, rows), 0)
            == lax.rem(idx_ref[...], tok)).astype(F32).astype(BF16)


def kernel(
    nx, nz, heads, tok, rows,
    idx_ref, k_ref, v_ref, q_ref, g_ref,
    dq_out, gkv,
    kvsend, kv, qb, gb, e_buf, dp_buf, m_buf, stats, stats_in, fin,
    dq_acc, dqb, dqr, dqs, part, rs_buf, rr_buf, ys_buf, yr_buf, gkv_send,
    loc_sem, xkv_s, xkv_r, xq_s, xq_r, xg_s, xg_r, y_s, y_r,
    ring_s, ring_r, sib_s, sib_r, join_s, join_r, red_s, red_r, yr_s, yr_r, xo_s, xo_r, xd_s, xd_r,
):
    width = heads * HEAD_DIM
    half = nz // 2
    hq = nx * tok
    nq = 2 * hq
    nk = 4 * nx * rows
    tq = min(256, hq)
    blk = lax.axis_index("blk")
    uly = lax.axis_index("uly")
    x = blk // nz
    z = blk % nz
    y = uly // 2
    c = uly % 2

    def along(by):
        return {"blk": x * nz + (z + nz + by) % nz}

    ypeer = {"uly": (1 - y) * 2 + c}
    sib = {"uly": y * 2 + (1 - c)}
    hop = [1, nx - 1] + list(range(2, nx - 1)) if nx > 2 else [1]

    def xpeer(j):
        return {"blk": ((x + j) % nx) * nz + z}

    def send(src, dst, s_sem, r_sem, dev):
        return pltpu.make_async_remote_copy(
            src_ref=src, dst_ref=dst, send_sem=s_sem, recv_sem=r_sem,
            device_id=dev, device_id_type=pl.DeviceIdType.MESH)

    def start(copies):
        for copy in copies:
            copy.start()

    def received(copies):
        for copy in copies:
            copy.wait_recv()

    def sent(copies):
        for copy in copies:
            copy.wait_send()

    barrier = pltpu.get_barrier_semaphore()
    others = [xpeer(j) for j in hop] + [along(1), along(-1), along(2), along(-2), ypeer, sib]
    for dev in others:
        pl.semaphore_signal(barrier, inc=1, device_id=dev, device_id_type=pl.DeviceIdType.MESH)

    hot = one_hot(idx_ref, tok, rows)
    for a, ref in enumerate((k_ref, v_ref)):
        for g in range(nx):
            for h in range(heads):
                col = (g * heads + h) * HEAD_DIM
                kvsend[g, h, a] = dot_tn(hot, ref[:, col:col + HEAD_DIM]).astype(BF16)

    pl.semaphore_wait(barrier, len(others))

    xrow = pl.ds(pl.multiple_of(x * rows, rows), rows)

    def token_rows(j):
        return pl.ds(pl.multiple_of((c * nx + (x + nx - j) % nx) * tok, tok), tok)

    def group_cols(j):
        return pl.ds(pl.multiple_of(((x + j) % nx) * width, width), width)

    kv_x = [send(kvsend.at[(x + j) % nx], kv.at[:, :, 0, y, xrow], xkv_s.at[j - 1], xkv_r.at[j - 1], xpeer(j))
            for j in hop]
    start(kv_x)
    kv_own = pltpu.make_async_copy(kvsend.at[x], kv.at[:, :, 0, y, xrow], loc_sem.at[0])
    kv_own.start()
    q_x = {j: [send(q_ref.at[:, group_cols(j)], qb.at[token_rows(0)], xq_s.at[j - 1], xq_r.at[j - 1], xpeer(j)),
               send(g_ref.at[:, group_cols(j)], gb.at[token_rows(0)], xg_s.at[j - 1], xg_r.at[j - 1], xpeer(j))]
           for j in hop}
    for j in hop:
        start(q_x[j])
    q_own = [pltpu.make_async_copy(q_ref.at[:, group_cols(0)], qb.at[token_rows(0)], loc_sem.at[1]),
             pltpu.make_async_copy(g_ref.at[:, group_cols(0)], gb.at[token_rows(0)], loc_sem.at[2])]
    start(q_own)

    share = {0: [send(q_ref.at[:, group_cols(0)], qb.at[token_rows(0)], sib_s.at[0, 0], sib_r.at[0, 0], sib),
                 send(g_ref.at[:, group_cols(0)], gb.at[token_rows(0)], sib_s.at[1, 0], sib_r.at[1, 0], sib)]}
    for j in hop:
        share[j] = [send(qb.at[token_rows(j)], qb.at[token_rows(j)], sib_s.at[0, j], sib_r.at[0, j], sib),
                    send(gb.at[token_rows(j)], gb.at[token_rows(j)], sib_s.at[1, j], sib_r.at[1, j], sib)]
    start(share[0])

    stats[...] = jnp.zeros_like(stats)
    for h in range(heads):
        stats[h, 0:1] = jnp.full((1, nq), -1e30, F32)
    dq_acc[...] = jnp.zeros_like(dq_acc)

    def ring(kind, s):
        def cut(slot, a):
            if kind == 0:
                return kv.at[1:heads, a, slot, y]
            return kv.at[0, a, slot]
        a_src, b_src, by = ((0, 0, s), (4, 5, s - 2))[s > 2]
        if s < half:
            ways = ((a_src, 2 * s, slice(None)), (b_src, 2 * s + 1, slice(None)))
        else:
            ways = ((a_src, 1, 0), (b_src, 1, 1))
        return [send(cut(src, a), cut(dst, a), ring_s.at[kind, w, s - 1], ring_r.at[kind, w, s - 1], along(way))
                for w, ((src, dst, a), way) in enumerate(zip(ways, (by, -by)))]

    def over_y(slot):
        return send(kv.at[1:heads, :, slot, y], kv.at[1:heads, :, slot, y], y_s.at[slot], y_r.at[slot], ypeer)

    def handle(s):
        slots = (2 * s, 2 * s + 1) if s < half else (1,)
        for kind in range(2):
            received(ring(kind, s))
            if s == 2 and half == 4:
                start(ring(kind, 3) + ring(kind, 4))
            if kind == 0:
                start([over_y(slot) for slot in slots])

    kv_own.wait()
    received(kv_x)
    start(ring(0, 2) + ring(0, 1))
    y_first = send(kv.at[0, :, 0, y], kv.at[0, :, 0, y], y_s.at[nz], y_r.at[nz], ypeer)
    start([y_first, over_y(0)])
    received([y_first])
    start(ring(1, 2) + ring(1, 1))
    for copy in q_own:
        copy.wait()
    if half > 2:
        handle(2)
    handle(1)
    for j in hop:
        received(q_x[j])
        start(share[j])

    def pass1(s, qh, h):
        lanes = pl.ds(pl.multiple_of(h * HEAD_DIM, HEAD_DIM), HEAD_DIM)
        keys = kv[h, 0, pl.ds(2 * s, 2)].reshape(nk, HEAD_DIM)
        vals = kv[h, 1, pl.ds(2 * s, 2)].reshape(nk, HEAD_DIM)
        for t in range(hq // tq):
            ts = pl.ds(pl.multiple_of(qh * hq + t * tq, tq), tq)
            sc = dot_nt(keys, qb[ts, lanes]) * (SCALE * LOG2E)
            dp = dot_nt(vals, gb[ts, lanes])
            m_old = stats[h, 0:1, ts]
            m_new = jnp.maximum(m_old, jnp.max(sc, axis=0, keepdims=True))
            e = jnp.exp2(sc - m_new)
            a = jnp.exp2(m_old - m_new)
            e_buf[s, h, :, ts] = e
            dp_buf[s, h, :, ts] = dp
            m_buf[s, h, 0:1, ts] = m_new
            stats[h, 0:1, ts] = m_new
            stats[h, 1:2, ts] = stats[h, 1:2, ts] * a + jnp.sum(e, axis=0, keepdims=True)
            stats[h, 2:3, ts] = stats[h, 2:3, ts] * a + jnp.sum(e * dp, axis=0, keepdims=True)

    def gather_step(i, carry):
        n = i // 2
        s = n + 1
        later = lax.rem(i, 2)
        for m in range(half - 1):
            @pl.when(i == 2 * m)
            def _():
                if m >= 1:
                    handle(m + 2)
                received([over_y(2 * m + 2), over_y(2 * m + 3)])

        @pl.when(i == 1)
        def _():
            for j in [0] + hop:
                received(share[j])

        def head(h, inner):
            pass1(s, lax.rem(c + later, 2), h)
            return inner
        lax.fori_loop(0, heads, head, 0)
        return carry

    lax.fori_loop(0, 2 * (half - 1), gather_step, 0)
    if half == 2:
        handle(2)

    def join(h):
        return send(stats.at[h], stats_in.at[h], join_s.at[h], join_r.at[h], sib)

    def last_head(h, carry):
        @pl.when(h == 1)
        def _():
            received([over_y(0), over_y(1)])

        def both(qh, inner):
            pass1(0, qh, h)
            return inner
        lax.fori_loop(0, 2, both, 0)
        join(h).start()
        return carry

    lax.fori_loop(0, heads, last_head, 0)

    def finish_stats(h):
        join(h).wait_recv()
        m1, m2 = stats[h, 0:1], stats_in[h, 0:1]
        m = jnp.maximum(m1, m2)
        a1, a2 = jnp.exp2(m1 - m), jnp.exp2(m2 - m)
        inv = 1.0 / (stats[h, 1:2] * a1 + stats_in[h, 1:2] * a2)
        fin[h, 0:1] = m
        fin[h, 1:2] = inv
        fin[h, 2:3] = (stats[h, 2:3] * a1 + stats_in[h, 2:3] * a2) * inv

    def pass2(s, h):
        lanes = pl.ds(pl.multiple_of(h * HEAD_DIM, HEAD_DIM), HEAD_DIM)
        keys = kv[h, 0, pl.ds(2 * s, 2)].reshape(nk, HEAD_DIM)
        dk = jnp.zeros((nk, HEAD_DIM), F32)
        dv = jnp.zeros((nk, HEAD_DIM), F32)
        for t in range(nq // tq):
            ts = slice(t * tq, (t + 1) * tq)
            r = jnp.exp2(m_buf[s, h, 0:1, ts] - fin[h, 0:1, ts]) * fin[h, 1:2, ts]
            p = e_buf[s, h, :, ts] * r
            ds = (p * (dp_buf[s, h, :, ts] - fin[h, 2:3, ts])).astype(BF16)
            dv = dv + dot_nn(p.astype(BF16), gb[ts, lanes])
            dk = dk + dot_nn(ds, qb[ts, lanes])
            dq_acc[h, :, ts] = dq_acc[h, :, ts] + dot_tn(keys, ds)
        part[h, 0, pl.ds(2 * s, 2)] = dk.astype(BF16).reshape(2, 2, nx * rows, HEAD_DIM)
        part[h, 1, pl.ds(2 * s, 2)] = dv.astype(BF16).reshape(2, 2, nx * rows, HEAD_DIM)

    def mine(kind, slot, a):
        return part.at[1:heads, a, slot, y] if kind == 0 else part.at[0, a, slot]

    def box(kind, w, n, a):
        return rs_buf.at[w, n, :, a] if kind == 0 else rr_buf.at[w, n, a]

    def reduce(kind, n):
        ways = []
        for w, sign in enumerate((1, -1)):
            if n == half:
                slot, a, by = 1, w, 2
            else:
                slot, a, by = 2 * n + 1 - w, slice(None), (n if n < 3 else 1)
            ways.append(send(mine(kind, slot, a), box(kind, w, n - 1, a),
                             red_s.at[kind, w, n - 1], red_r.at[kind, w, n - 1], along(sign * by)))
        return ways

    def reduce_y(slot):
        return send(part.at[1:heads, :, slot, 1 - y], ys_buf.at[slot], yr_s.at[slot], yr_r.at[slot], ypeer)

    def add_y(slot):
        reduce_y(slot).wait_recv()
        part[1:heads, :, slot, y] = (part[1:heads, :, slot, y].astype(F32) + ys_buf[slot].astype(F32)).astype(BF16)

    def add_boxes(kind):
        received(reduce(kind, 3) + reduce(kind, 4))
        for w in range(2):
            slot = 5 - w
            for a in range(2):
                if kind == 0:
                    total = part[1:heads, a, slot, y].astype(F32) + rs_buf[w, 2, :, a].astype(F32)
                    if a == w:
                        total = total + rs_buf[w, 3, :, a].astype(F32)
                    part[1:heads, a, slot, y] = total.astype(BF16)
                else:
                    total = part[0, a, slot].astype(F32) + rr_buf[w, 2, a].astype(F32)
                    if a == w:
                        total = total + rr_buf[w, 3, a].astype(F32)
                    part[0, a, slot] = total.astype(BF16)

    order = [3, 4, 1, 2] if half == 4 else [2, 1]

    def pair_of(t):
        return lax.rem(t + 3, 4) if half == 4 else t

    def produce(t):
        s = pair_of(t)

        def head(n, carry):
            h = lax.rem(n + 1, heads)

            @pl.when(t == 0)
            def _():
                finish_stats(h)
            pass2(s, h)

            @pl.when(n == heads - 2)
            def _():
                for k, place in enumerate(order):
                    @pl.when(t == k)
                    def _():
                        start([reduce_y(slot) for slot in ((2 * place + 1, 2 * place) if place < half else (1,))])
            return carry
        lax.fori_loop(0, heads, head, 0)
        for k, place in enumerate(order):
            if place != 2 or half == 2:
                @pl.when(t == k)
                def _():
                    start(reduce(1, place))

    def pass_on(t):
        for k, place in enumerate(order):
            @pl.when(t == k)
            def _():
                for slot in ((2 * place + 1, 2 * place) if place < half else (1,)):
                    add_y(slot)
                if place == 2 and half == 4:
                    for kind in (1, 0):
                        add_boxes(kind)
                        start(reduce(kind, 2))
                else:
                    start(reduce(0, place))

    dq_sib = send(dqb.at[1 - c], dqr, sib_s.at[0, nx], sib_r.at[0, nx], sib)

    def reduce_step(t, carry):
        @pl.when(t < half)
        def _():
            produce(t)

        @pl.when(t == half)
        def _():
            start([reduce_y(0)])
            for h in range(heads):
                for cc in range(2):
                    for xs in range(nx):
                        at = (cc * nx + xs) * tok
                        dqb[cc, xs, :, h * HEAD_DIM:(h + 1) * HEAD_DIM] = (
                            jnp.transpose(dq_acc[h, :, at:at + tok]) * SCALE).astype(BF16)
            dq_sib.start()

        @pl.when(t > 0)
        def _():
            pass_on(t - 1)
        return carry

    lax.fori_loop(0, half + 1, reduce_step, 0)

    dq_sib.wait()
    for xs in range(nx):
        dqs[xs] = (dqb[c, xs].astype(F32) + dqr[xs].astype(F32)).astype(BF16)
    dq_x = [send(dqs.at[(x + j) % nx], dq_out.at[:, group_cols(0)], xd_s.at[j - 1], xd_r.at[j - 1], xpeer(j))
            for j in hop]
    start(dq_x)
    dq_own = pltpu.make_async_copy(dqs.at[x], dq_out.at[:, group_cols(0)], loc_sem.at[3])
    dq_own.start()

    received(reduce(1, 1) + reduce(1, 2))

    def total_r(a):
        total = part[0, a, 0].astype(F32)
        for w in range(2):
            total = total + rr_buf[w, 0, a].astype(F32)
            if half == 4 or a == w:
                total = total + rr_buf[w, 1, a].astype(F32)
        return total

    def total_s(h, a):
        total = part[h, a, 0, y].astype(F32) + ys_buf[0, h - 1, a].astype(F32)
        for w in range(2):
            total = total + rs_buf[w, 0, h - 1, a].astype(F32)
            if half == 4 or a == w:
                total = total + rs_buf[w, 1, h - 1, a].astype(F32)
        return total

    for a in range(2):
        part[0, a, 0] = total_r(a).astype(BF16)
    y_last = send(part.at[0, :, 0, 1 - y], yr_buf, yr_s.at[nz], yr_r.at[nz], ypeer)
    y_last.start()

    def put(h, a, total):
        if a == 0:
            total = total * SCALE
        total = total.astype(BF16)
        for xs in range(nx):
            gkv_send[xs, h, a] = total[xs * rows:(xs + 1) * rows]

    reduce_y(0).wait_recv()
    received(reduce(0, 1) + reduce(0, 2))
    for h in range(1, heads):
        for a in range(2):
            put(h, a, total_s(h, a))
    y_last.wait_recv()
    for a in range(2):
        put(0, a, part[0, a, 0, y].astype(F32) + yr_buf[a].astype(F32))
    out_x = [send(gkv_send.at[(x + j) % nx], gkv.at[x], xo_s.at[j - 1], xo_r.at[j - 1], xpeer(j)) for j in hop]
    start(out_x)
    out_own = pltpu.make_async_copy(gkv_send.at[x], gkv.at[x], loc_sem.at[4])
    out_own.start()

    sent(kv_x)
    for j in hop:
        sent(q_x[j])
    for j in [0] + hop:
        sent(share[j])
    for kind in range(2):
        for s in range(1, half + 1):
            sent(ring(kind, s) + reduce(kind, s))
    for slot in range(nz):
        sent([over_y(slot), reduce_y(slot)])
    sent([y_first, y_last])
    for h in range(heads):
        join(h).wait_send()
    dq_own.wait()
    for copy in dq_x:
        copy.wait()
    out_own.wait()
    for copy in out_x:
        copy.wait()


def place(nx, heads, tok, rows, idx_ref, dq_ref, gkv_ref, dq_out, dk_out, dv_out):
    dq_out[...] = dq_ref[...]
    hot = one_hot(idx_ref, tok, rows)
    for a, ref in enumerate((dk_out, dv_out)):
        for g in range(nx):
            for h in range(heads):
                col = (g * heads + h) * HEAD_DIM
                ref[:, col:col + HEAD_DIM] = dot_nn(hot, gkv_ref[g, h, a]).astype(BF16)


def per_device(nx, nz, queries, key_input, value_input, grad_out, keep_index):
    tok, columns = queries.shape
    rows = keep_index.shape[0]
    heads = columns // HEAD_DIM // nx
    width = heads * HEAD_DIM
    half = nz // 2
    nq = 2 * nx * tok
    nk = 4 * nx * rows
    slab = (nx * rows, HEAD_DIM)
    dma = pltpu.SemaphoreType.DMA
    vmem = pltpu.VMEM
    out = jax.ShapeDtypeStruct((tok, columns), BF16)
    compact = (nx, heads, 2, rows, HEAD_DIM)
    in_vmem = pl.BlockSpec(memory_space=pltpu.VMEM)
    in_any = pl.BlockSpec(memory_space=pl.ANY)
    flops = 2 * 6 * heads * nq * (half * nk) * HEAD_DIM
    index = keep_index.reshape(1, rows)
    dq, gkv = pl.pallas_call(
        functools.partial(kernel, nx, nz, heads, tok, rows),
        out_shape=(out, jax.ShapeDtypeStruct(compact, BF16)),
        in_specs=[in_vmem, in_vmem, in_vmem, in_any, in_any],
        out_specs=(in_vmem, in_vmem),
        scratch_shapes=[
            vmem(compact, BF16),
            vmem((heads, 2, nz, 2) + slab, BF16),
            vmem((nq, width), BF16),
            vmem((nq, width), BF16),
            vmem((half, heads, nk, nq), F32),
            vmem((half, heads, nk, nq), F32),
            vmem((half, heads, 8, nq), F32),
            vmem((heads, 8, nq), F32),
            vmem((heads, 8, nq), F32),
            vmem((heads, 8, nq), F32),
            vmem((heads, HEAD_DIM, nq), F32),
            vmem((2, nx, tok, width), BF16),
            vmem((nx, tok, width), BF16),
            vmem((nx, tok, width), BF16),
            vmem((heads, 2, nz, 2) + slab, BF16),
            vmem((2, half, heads - 1, 2) + slab, BF16),
            vmem((2, half, 2, 2) + slab, BF16),
            vmem((nz, heads - 1, 2) + slab, BF16),
            vmem((2,) + slab, BF16),
            vmem(compact, BF16),
            dma((5,)),
            dma((nx - 1,)), dma((nx - 1,)),
            dma((nx - 1,)), dma((nx - 1,)),
            dma((nx - 1,)), dma((nx - 1,)),
            dma((nz + 1,)), dma((nz + 1,)),
            dma((2, 2, half)), dma((2, 2, half)),
            dma((2, nx + 1)), dma((2, nx + 1)),
            dma((heads,)), dma((heads,)),
            dma((2, 2, half)), dma((2, 2, half)),
            dma((nz + 1,)), dma((nz + 1,)),
            dma((nx - 1,)), dma((nx - 1,)),
            dma((nx - 1,)), dma((nx - 1,)),
        ],
        compiler_params=pltpu.CompilerParams(
            collective_id=0, has_side_effects=True, vmem_limit_bytes=56 * 2 ** 20),
        cost_estimate=pl.CostEstimate(
            flops=flops, bytes_accessed=7 * tok * columns * 2, transcendentals=heads * nq * half * nk),
    )(index, key_input, value_input, queries, grad_out)
    return pl.pallas_call(
        functools.partial(place, nx, heads, tok, rows),
        out_shape=(out, out, out),
        in_specs=[in_vmem] * 3,
        out_specs=(in_vmem,) * 3,
    )(index, dq, gkv)


def build(mesh, nx, nz):
    rows_spec = P(("rep", "blk", "uly"), None)
    return jax.shard_map(
        functools.partial(per_device, nx, nz), mesh=mesh,
        in_specs=(rows_spec,) * 4 + (P(("rep", "blk", "uly")),),
        out_specs=(rows_spec,) * 3, check_vma=False)


def solution(mesh):
    return build(mesh, 4, 8)
```

```python
import functools

import jax
import jax.numpy as jnp
from jax import lax
from jax.experimental import pallas as pl
from jax.experimental.pallas import tpu as pltpu
from jax.sharding import PartitionSpec as P

HEAD_DIM = 128
CELL = 8
SCALE = HEAD_DIM ** -0.5
LOG2E = 1.4426950408889634
F32 = jnp.float32
BF16 = jnp.bfloat16
ULY = 4


def dot_nn(a, b):
    return lax.dot_general(a, b, (((1,), (0,)), ((), ())), preferred_element_type=F32)


def dot_nt(a, b):
    return lax.dot_general(a, b, (((1,), (1,)), ((), ())), preferred_element_type=F32)


def dot_tn(a, b):
    return lax.dot_general(a, b, (((0,), (0,)), ((), ())), preferred_element_type=F32)


def one_hot(idx_ref, tok, rows):
    return (lax.broadcasted_iota(jnp.int32, (tok, rows), 0)
            == lax.rem(idx_ref[...], tok)).astype(F32).astype(BF16)


def kernel(
    nx, nz, heads, tok, rows,
    idx_ref, k_ref, v_ref, q_ref, g_ref,
    dq_out, gkv,
    kvsend, kv, qb, gb, e_buf, dp_buf, m_buf, stats, stats_in, fin,
    dq_acc, dqb, dqr, dqs, part, rs_buf, rr_buf, ys_buf, yr_buf, gkv_send,
    loc_sem, xkv_s, xkv_r, xq_s, xq_r, xg_s, xg_r, y_s, y_r,
    ring_s, ring_r, sib_s, sib_r, join_s, join_r, red_s, red_r, yr_s, yr_r, xo_s, xo_r, xd_s, xd_r,
):
    width = heads * HEAD_DIM
    half = nz // 2
    hq = nx * tok
    nq = 2 * hq
    nk = 4 * nx * rows
    tq = min(256, hq)
    blk = lax.axis_index("blk")
    uly = lax.axis_index("uly")
    x = blk // nz
    z = blk % nz
    y = uly // 2
    c = uly % 2

    def along(by):
        return {"blk": x * nz + (z + nz + by) % nz}

    ypeer = {"uly": (1 - y) * 2 + c}
    sib = {"uly": y * 2 + (1 - c)}
    hop = [1, nx - 1] + list(range(2, nx - 1)) if nx > 2 else [1]

    def xpeer(j):
        return {"blk": ((x + j) % nx) * nz + z}

    def send(src, dst, s_sem, r_sem, dev):
        return pltpu.make_async_remote_copy(
            src_ref=src, dst_ref=dst, send_sem=s_sem, recv_sem=r_sem,
            device_id=dev, device_id_type=pl.DeviceIdType.MESH)

    def start(copies):
        for copy in copies:
            copy.start()

    def received(copies):
        for copy in copies:
            copy.wait_recv()

    def sent(copies):
        for copy in copies:
            copy.wait_send()

    barrier = pltpu.get_barrier_semaphore()
    others = [xpeer(j) for j in hop] + [along(1), along(-1), along(2), along(-2), ypeer, sib]
    for dev in others:
        pl.semaphore_signal(barrier, inc=1, device_id=dev, device_id_type=pl.DeviceIdType.MESH)

    hot = one_hot(idx_ref, tok, rows)
    for a, ref in enumerate((k_ref, v_ref)):
        for g in range(nx):
            for h in range(heads):
                col = (g * heads + h) * HEAD_DIM
                kvsend[g, h, a] = dot_tn(hot, ref[:, col:col + HEAD_DIM]).astype(BF16)

    pl.semaphore_wait(barrier, len(others))

    xrow = pl.ds(pl.multiple_of(x * rows, rows), rows)

    def token_rows(j):
        return pl.ds(pl.multiple_of((c * nx + (x + nx - j) % nx) * tok, tok), tok)

    def group_cols(j):
        return pl.ds(pl.multiple_of(((x + j) % nx) * width, width), width)

    kv_x = [send(kvsend.at[(x + j) % nx], kv.at[:, :, 0, y, xrow], xkv_s.at[j - 1], xkv_r.at[j - 1], xpeer(j))
            for j in hop]
    start(kv_x)
    kv_own = pltpu.make_async_copy(kvsend.at[x], kv.at[:, :, 0, y, xrow], loc_sem.at[0])
    kv_own.start()
    q_x = {j: [send(q_ref.at[:, group_cols(j)], qb.at[token_rows(0)], xq_s.at[j - 1], xq_r.at[j - 1], xpeer(j)),
               send(g_ref.at[:, group_cols(j)], gb.at[token_rows(0)], xg_s.at[j - 1], xg_r.at[j - 1], xpeer(j))]
           for j in hop}
    for j in hop:
        start(q_x[j])
    q_own = [pltpu.make_async_copy(q_ref.at[:, group_cols(0)], qb.at[token_rows(0)], loc_sem.at[1]),
             pltpu.make_async_copy(g_ref.at[:, group_cols(0)], gb.at[token_rows(0)], loc_sem.at[2])]
    start(q_own)

    share = {0: [send(q_ref.at[:, group_cols(0)], qb.at[token_rows(0)], sib_s.at[0, 0], sib_r.at[0, 0], sib),
                 send(g_ref.at[:, group_cols(0)], gb.at[token_rows(0)], sib_s.at[1, 0], sib_r.at[1, 0], sib)]}
    for j in hop:
        share[j] = [send(qb.at[token_rows(j)], qb.at[token_rows(j)], sib_s.at[0, j], sib_r.at[0, j], sib),
                    send(gb.at[token_rows(j)], gb.at[token_rows(j)], sib_s.at[1, j], sib_r.at[1, j], sib)]
    start(share[0])

    stats[...] = jnp.zeros_like(stats)
    for h in range(heads):
        stats[h, 0:1] = jnp.full((1, nq), -1e30, F32)
    dq_acc[...] = jnp.zeros_like(dq_acc)

    def ring(kind, s):
        def cut(slot, a):
            if kind == 0:
                return kv.at[1:heads, a, slot, y]
            return kv.at[0, a, slot]
        a_src, b_src, by = ((0, 0, 1), (2, 3, 1), (4, 5, 1), (4, 5, 2))[s - 1]
        if s < half:
            ways = ((a_src, 2 * s, slice(None)), (b_src, 2 * s + 1, slice(None)))
        else:
            ways = ((a_src, 1, 0), (b_src, 1, 1))
        return [send(cut(src, a), cut(dst, a), ring_s.at[kind, w, s - 1], ring_r.at[kind, w, s - 1], along(way))
                for w, ((src, dst, a), way) in enumerate(zip(ways, (by, -by)))]

    def over_y(slot):
        return send(kv.at[1:heads, :, slot, y], kv.at[1:heads, :, slot, y], y_s.at[slot], y_r.at[slot], ypeer)

    def handle(s):
        for kind in range(2):
            onward = [ring(kind, n) for n in ((2,), (3, 4), (), ())[s - 1]]
            for w, copy in enumerate(ring(kind, s)):
                copy.wait_recv()
                start([copies[w] for copies in onward])
                if kind == 0 and s < half:
                    over_y(2 * s + w).start()
            if kind == 0 and s == half:
                over_y(1).start()

    kv_own.wait()
    received(kv_x)
    start(ring(0, 1))
    y_first = send(kv.at[0, :, 0, y], kv.at[0, :, 0, y], y_s.at[nz], y_r.at[nz], ypeer)
    start([y_first, over_y(0)])
    received([y_first])
    start(ring(1, 1))
    for copy in q_own:
        copy.wait()
    handle(1)
    for j in hop:
        received(q_x[j])
        start(share[j])
    handle(2)

    def pass1(s, qh, h):
        lanes = pl.ds(pl.multiple_of(h * HEAD_DIM, HEAD_DIM), HEAD_DIM)
        keys = kv[h, 0, pl.ds(2 * s, 2)].reshape(nk, HEAD_DIM)
        vals = kv[h, 1, pl.ds(2 * s, 2)].reshape(nk, HEAD_DIM)
        for t in range(hq // tq):
            ts = pl.ds(pl.multiple_of(qh * hq + t * tq, tq), tq)
            sc = dot_nt(keys, qb[ts, lanes]) * (SCALE * LOG2E)
            dp = dot_nt(vals, gb[ts, lanes])
            m_old = stats[h, 0:1, ts]
            m_new = jnp.maximum(m_old, jnp.max(sc, axis=0, keepdims=True))
            e = jnp.exp2(sc - m_new)
            a = jnp.exp2(m_old - m_new)
            e_buf[s, h, :, ts] = e
            dp_buf[s, h, :, ts] = dp
            m_buf[s, h, 0:1, ts] = m_new
            stats[h, 0:1, ts] = m_new
            stats[h, 1:2, ts] = stats[h, 1:2, ts] * a + jnp.sum(e, axis=0, keepdims=True)
            stats[h, 2:3, ts] = stats[h, 2:3, ts] * a + jnp.sum(e * dp, axis=0, keepdims=True)

    def gather_step(i, carry):
        n = i // 2
        s = n + 1
        later = lax.rem(i, 2)
        for m in range(half - 1):
            @pl.when(i == 2 * m)
            def _():
                if m >= 1:
                    handle(m + 2)
                received([over_y(2 * m + 2), over_y(2 * m + 3)])

        @pl.when(i == 1)
        def _():
            for j in [0] + hop:
                received(share[j])

        def head(h, inner):
            pass1(s, lax.rem(c + later, 2), h)
            return inner
        lax.fori_loop(0, heads, head, 0)
        return carry

    lax.fori_loop(0, 2 * (half - 1), gather_step, 0)
    def join(h):
        return send(stats.at[h], stats_in.at[h], join_s.at[h], join_r.at[h], sib)

    def last_head(h, carry):
        @pl.when(h == 1)
        def _():
            received([over_y(0), over_y(1)])

        def both(qh, inner):
            pass1(0, qh, h)
            return inner
        lax.fori_loop(0, 2, both, 0)
        join(h).start()
        return carry

    lax.fori_loop(0, heads, last_head, 0)

    def finish_stats(h):
        join(h).wait_recv()
        m1, m2 = stats[h, 0:1], stats_in[h, 0:1]
        m = jnp.maximum(m1, m2)
        a1, a2 = jnp.exp2(m1 - m), jnp.exp2(m2 - m)
        inv = 1.0 / (stats[h, 1:2] * a1 + stats_in[h, 1:2] * a2)
        fin[h, 0:1] = m
        fin[h, 1:2] = inv
        fin[h, 2:3] = (stats[h, 2:3] * a1 + stats_in[h, 2:3] * a2) * inv

    def pass2(s, h):
        lanes = pl.ds(pl.multiple_of(h * HEAD_DIM, HEAD_DIM), HEAD_DIM)
        keys = kv[h, 0, pl.ds(2 * s, 2)].reshape(nk, HEAD_DIM)
        dk = jnp.zeros((nk, HEAD_DIM), F32)
        dv = jnp.zeros((nk, HEAD_DIM), F32)
        for t in range(nq // tq):
            ts = slice(t * tq, (t + 1) * tq)
            r = jnp.exp2(m_buf[s, h, 0:1, ts] - fin[h, 0:1, ts]) * fin[h, 1:2, ts]
            p = e_buf[s, h, :, ts] * r
            ds = (p * (dp_buf[s, h, :, ts] - fin[h, 2:3, ts])).astype(BF16)
            dv = dv + dot_nn(p.astype(BF16), gb[ts, lanes])
            dk = dk + dot_nn(ds, qb[ts, lanes])
            dq_acc[h, :, ts] = dq_acc[h, :, ts] + dot_tn(keys, ds)
        part[h, 0, pl.ds(2 * s, 2)] = dk.astype(BF16).reshape(2, 2, nx * rows, HEAD_DIM)
        part[h, 1, pl.ds(2 * s, 2)] = dv.astype(BF16).reshape(2, 2, nx * rows, HEAD_DIM)

    def mine(kind, slot, a):
        return part.at[1:heads, a, slot, y] if kind == 0 else part.at[0, a, slot]

    def box(kind, w, n, a):
        return rs_buf.at[w, n, :, a] if kind == 0 else rr_buf.at[w, n, a]

    def reduce(kind, n):
        ways = []
        for w, sign in enumerate((1, -1)):
            if n == half:
                slot, a, by = 1, w, 2
            else:
                slot, a, by = 2 * n + 1 - w, slice(None), 1
            ways.append(send(mine(kind, slot, a), box(kind, w, n - 1, a),
                             red_s.at[kind, w, n - 1], red_r.at[kind, w, n - 1], along(sign * by)))
        return ways

    def reduce_y(slot):
        return send(part.at[1:heads, :, slot, 1 - y], ys_buf.at[slot], yr_s.at[slot], yr_r.at[slot], ypeer)

    def add_y(slot):
        reduce_y(slot).wait_recv()
        part[1:heads, :, slot, y] = (part[1:heads, :, slot, y].astype(F32) + ys_buf[slot].astype(F32)).astype(BF16)

    def relay(kind, n):
        for w in range(2):
            slot = 2 * n + 1 - w
            if kind == 0:
                add_y(slot)
            received([reduce(kind, n + 1)[w]] + ([reduce(kind, 4)[w]] if n == 2 else []))
            for a in range(2):
                far = n == 2 and a == w
                if kind == 0:
                    total = part[1:heads, a, slot, y].astype(F32) + rs_buf[w, n, :, a].astype(F32)
                    if far:
                        total = total + rs_buf[w, 3, :, a].astype(F32)
                    part[1:heads, a, slot, y] = total.astype(BF16)
                else:
                    total = part[0, a, slot].astype(F32) + rr_buf[w, n, a].astype(F32)
                    if far:
                        total = total + rr_buf[w, 3, a].astype(F32)
                    part[0, a, slot] = total.astype(BF16)
            reduce(kind, n)[w].start()

    order = [4, 3, 2, 1]

    def produce(t):
        s = lax.rem(half - t, half)

        def head(n, carry):
            h = lax.rem(n + 1, heads)

            @pl.when(t == 0)
            def _():
                finish_stats(h)
            pass2(s, h)

            @pl.when(n == heads - 2)
            def _():
                for k, place in enumerate(order):
                    @pl.when(t == k)
                    def _():
                        start([reduce_y(slot) for slot in ((2 * place + 1, 2 * place) if place < half else (1,))])
            return carry
        lax.fori_loop(0, heads, head, 0)
        for k, place in enumerate(order):
            if place > 2:
                @pl.when(t == k)
                def _():
                    start(reduce(1, place))

    def pass_on(t):
        for k, place in enumerate(order):
            @pl.when(t == k)
            def _():
                if place < 3:
                    relay(1, place)
                    relay(0, place)
                elif place == 3:
                    for w in range(2):
                        add_y(7 - w)
                        reduce(0, 3)[w].start()
                else:
                    add_y(1)
                    start(reduce(0, 4))

    dq_sib = send(dqb.at[1 - c], dqr, sib_s.at[0, nx], sib_r.at[0, nx], sib)

    def reduce_step(t, carry):
        @pl.when(t < half)
        def _():
            produce(t)

        @pl.when(t == half)
        def _():
            start([reduce_y(0)])
            for h in range(heads):
                for cc in range(2):
                    for xs in range(nx):
                        at = (cc * nx + xs) * tok
                        dqb[cc, xs, :, h * HEAD_DIM:(h + 1) * HEAD_DIM] = (
                            jnp.transpose(dq_acc[h, :, at:at + tok]) * SCALE).astype(BF16)
            dq_sib.start()

        @pl.when(t > 0)
        def _():
            pass_on(t - 1)
        return carry

    lax.fori_loop(0, half + 1, reduce_step, 0)

    dq_sib.wait()
    for xs in range(nx):
        dqs[xs] = (dqb[c, xs].astype(F32) + dqr[xs].astype(F32)).astype(BF16)
    dq_x = [send(dqs.at[(x + j) % nx], dq_out.at[:, group_cols(0)], xd_s.at[j - 1], xd_r.at[j - 1], xpeer(j))
            for j in hop]
    start(dq_x)
    dq_own = pltpu.make_async_copy(dqs.at[x], dq_out.at[:, group_cols(0)], loc_sem.at[3])
    dq_own.start()

    received(reduce(1, 1))

    def total_r(a):
        total = part[0, a, 0].astype(F32)
        for w in range(2):
            total = total + rr_buf[w, 0, a].astype(F32)
        return total

    def total_s(h, a):
        total = part[h, a, 0, y].astype(F32) + ys_buf[0, h - 1, a].astype(F32)
        for w in range(2):
            total = total + rs_buf[w, 0, h - 1, a].astype(F32)
        return total

    for a in range(2):
        part[0, a, 0] = total_r(a).astype(BF16)
    y_last = send(part.at[0, :, 0, 1 - y], yr_buf, yr_s.at[nz], yr_r.at[nz], ypeer)
    y_last.start()

    def put(h, a, total):
        if a == 0:
            total = total * SCALE
        total = total.astype(BF16)
        for xs in range(nx):
            gkv_send[xs, h, a] = total[xs * rows:(xs + 1) * rows]

    reduce_y(0).wait_recv()
    received(reduce(0, 1))
    for h in range(1, heads):
        for a in range(2):
            put(h, a, total_s(h, a))
    y_last.wait_recv()
    for a in range(2):
        put(0, a, part[0, a, 0, y].astype(F32) + yr_buf[a].astype(F32))
    out_x = [send(gkv_send.at[(x + j) % nx], gkv.at[x], xo_s.at[j - 1], xo_r.at[j - 1], xpeer(j)) for j in hop]
    start(out_x)
    out_own = pltpu.make_async_copy(gkv_send.at[x], gkv.at[x], loc_sem.at[4])
    out_own.start()

    sent(kv_x)
    for j in hop:
        sent(q_x[j])
    for j in [0] + hop:
        sent(share[j])
    for kind in range(2):
        for s in range(1, half + 1):
            sent(ring(kind, s) + reduce(kind, s))
    for slot in range(nz):
        sent([over_y(slot), reduce_y(slot)])
    sent([y_first, y_last])
    for h in range(heads):
        join(h).wait_send()
    dq_own.wait()
    for copy in dq_x:
        copy.wait()
    out_own.wait()
    for copy in out_x:
        copy.wait()


def place(nx, heads, tok, rows, idx_ref, dq_ref, gkv_ref, dq_out, dk_out, dv_out):
    dq_out[...] = dq_ref[...]
    hot = one_hot(idx_ref, tok, rows)
    for a, ref in enumerate((dk_out, dv_out)):
        for g in range(nx):
            for h in range(heads):
                col = (g * heads + h) * HEAD_DIM
                ref[:, col:col + HEAD_DIM] = dot_nn(hot, gkv_ref[g, h, a]).astype(BF16)


def per_device(nx, nz, queries, key_input, value_input, grad_out, keep_index):
    tok, columns = queries.shape
    rows = keep_index.shape[0]
    heads = columns // HEAD_DIM // nx
    width = heads * HEAD_DIM
    half = nz // 2
    nq = 2 * nx * tok
    nk = 4 * nx * rows
    slab = (nx * rows, HEAD_DIM)
    dma = pltpu.SemaphoreType.DMA
    vmem = pltpu.VMEM
    out = jax.ShapeDtypeStruct((tok, columns), BF16)
    compact = (nx, heads, 2, rows, HEAD_DIM)
    in_vmem = pl.BlockSpec(memory_space=pltpu.VMEM)
    in_any = pl.BlockSpec(memory_space=pl.ANY)
    flops = 2 * 6 * heads * nq * (half * nk) * HEAD_DIM
    index = keep_index.reshape(1, rows)
    dq, gkv = pl.pallas_call(
        functools.partial(kernel, nx, nz, heads, tok, rows),
        out_shape=(out, jax.ShapeDtypeStruct(compact, BF16)),
        in_specs=[in_vmem, in_vmem, in_vmem, in_any, in_any],
        out_specs=(in_vmem, in_vmem),
        scratch_shapes=[
            vmem(compact, BF16),
            vmem((heads, 2, nz, 2) + slab, BF16),
            vmem((nq, width), BF16),
            vmem((nq, width), BF16),
            vmem((half, heads, nk, nq), F32),
            vmem((half, heads, nk, nq), F32),
            vmem((half, heads, 8, nq), F32),
            vmem((heads, 8, nq), F32),
            vmem((heads, 8, nq), F32),
            vmem((heads, 8, nq), F32),
            vmem((heads, HEAD_DIM, nq), F32),
            vmem((2, nx, tok, width), BF16),
            vmem((nx, tok, width), BF16),
            vmem((nx, tok, width), BF16),
            vmem((heads, 2, nz, 2) + slab, BF16),
            vmem((2, half, heads - 1, 2) + slab, BF16),
            vmem((2, half, 2, 2) + slab, BF16),
            vmem((nz, heads - 1, 2) + slab, BF16),
            vmem((2,) + slab, BF16),
            vmem(compact, BF16),
            dma((5,)),
            dma((nx - 1,)), dma((nx - 1,)),
            dma((nx - 1,)), dma((nx - 1,)),
            dma((nx - 1,)), dma((nx - 1,)),
            dma((nz + 1,)), dma((nz + 1,)),
            dma((2, 2, half)), dma((2, 2, half)),
            dma((2, nx + 1)), dma((2, nx + 1)),
            dma((heads,)), dma((heads,)),
            dma((2, 2, half)), dma((2, 2, half)),
            dma((nz + 1,)), dma((nz + 1,)),
            dma((nx - 1,)), dma((nx - 1,)),
            dma((nx - 1,)), dma((nx - 1,)),
        ],
        compiler_params=pltpu.CompilerParams(
            collective_id=0, has_side_effects=True, vmem_limit_bytes=56 * 2 ** 20),
        cost_estimate=pl.CostEstimate(
            flops=flops, bytes_accessed=7 * tok * columns * 2, transcendentals=heads * nq * half * nk),
    )(index, key_input, value_input, queries, grad_out)
    return pl.pallas_call(
        functools.partial(place, nx, heads, tok, rows),
        out_shape=(out, out, out),
        in_specs=[in_vmem] * 3,
        out_specs=(in_vmem,) * 3,
    )(index, dq, gkv)


def build(mesh, nx, nz):
    rows_spec = P(("rep", "blk", "uly"), None)
    return jax.shard_map(
        functools.partial(per_device, nx, nz), mesh=mesh,
        in_specs=(rows_spec,) * 4 + (P(("rep", "blk", "uly")),),
        out_specs=(rows_spec,) * 3, check_vma=False)


def solution(mesh):
    return build(mesh, 4, 8)
```

```python
import functools

import jax
import jax.numpy as jnp
from jax import lax
from jax.experimental import pallas as pl
from jax.experimental.pallas import tpu as pltpu
from jax.sharding import PartitionSpec as P

HEAD_DIM = 128
CELL = 8
SCALE = HEAD_DIM ** -0.5
LOG2E = 1.4426950408889634
F32 = jnp.float32
BF16 = jnp.bfloat16
ULY = 4


def dot_nn(a, b):
    return lax.dot_general(a, b, (((1,), (0,)), ((), ())), preferred_element_type=F32)


def dot_nt(a, b):
    return lax.dot_general(a, b, (((1,), (1,)), ((), ())), preferred_element_type=F32)


def dot_tn(a, b):
    return lax.dot_general(a, b, (((0,), (0,)), ((), ())), preferred_element_type=F32)


def one_hot(idx_ref, tok, rows):
    return (lax.broadcasted_iota(jnp.int32, (tok, rows), 0)
            == lax.rem(idx_ref[...], tok)).astype(F32).astype(BF16)


def kernel(
    nx, nz, heads, tok, rows,
    idx_ref, k_ref, v_ref, q_ref, g_ref,
    dq_out, gkv,
    kvsend, kv, qb, gb, e_buf, dp_buf, m_buf, stats, stats_in, fin,
    dq_acc, dqb, dqr, dqs, part, rs_buf, rr_buf, ys_buf, gkv_send, zero_send, zero,
    loc_sem, xkv_s, xkv_r, xq_s, xq_r, xg_s, xg_r, y_s, y_r,
    ring_s, ring_r, sib_s, sib_r, join_s, join_r, red_s, red_r, yr_s, yr_r, xo_s, xo_r, xd_s, xd_r,
):
    width = heads * HEAD_DIM
    half = nz // 2
    hq = nx * tok
    nq = 2 * hq
    nk = 4 * nx * rows
    tq = min(256, hq)
    blk = lax.axis_index("blk")
    uly = lax.axis_index("uly")
    x = blk // nz
    z = blk % nz
    y = uly // 2
    c = uly % 2

    def along(by):
        return {"blk": x * nz + (z + nz + by) % nz}

    ypeer = {"uly": (1 - y) * 2 + c}
    sib = {"uly": y * 2 + (1 - c)}
    hop = [1, nx - 1] + list(range(2, nx - 1)) if nx > 2 else [1]

    def xpeer(j):
        return {"blk": ((x + j) % nx) * nz + z}

    def crossed(j):
        return {"blk": ((x + j) % nx) * nz + z, "uly": (1 - y) * 2 + c}

    def send(src, dst, s_sem, r_sem, dev):
        return pltpu.make_async_remote_copy(
            src_ref=src, dst_ref=dst, send_sem=s_sem, recv_sem=r_sem,
            device_id=dev, device_id_type=pl.DeviceIdType.MESH)

    def start(copies):
        for copy in copies:
            copy.start()

    def received(copies):
        for copy in copies:
            copy.wait_recv()

    def sent(copies):
        for copy in copies:
            copy.wait_send()

    barrier = pltpu.get_barrier_semaphore()
    others = [xpeer(j) for j in hop] + [crossed(j) for j in hop] + [along(1), along(-1), along(2), along(-2), ypeer, sib]
    for dev in others:
        pl.semaphore_signal(barrier, inc=1, device_id=dev, device_id_type=pl.DeviceIdType.MESH)

    hot = one_hot(idx_ref, tok, rows)
    for a, ref in enumerate((k_ref, v_ref)):
        for g in range(nx):
            for h in range(heads):
                col = (g * heads + h) * HEAD_DIM
                kvsend[g, h, a] = dot_tn(hot, ref[:, col:col + HEAD_DIM]).astype(BF16)

    pl.semaphore_wait(barrier, len(others))

    xrow = pl.ds(pl.multiple_of(x * rows, rows), rows)

    def token_rows(j):
        return pl.ds(pl.multiple_of((c * nx + (x + nx - j) % nx) * tok, tok), tok)

    def group_cols(j):
        return pl.ds(pl.multiple_of(((x + j) % nx) * width, width), width)

    kv_x = [send(kvsend.at[(x + j) % nx], kv.at[:, :, 0, y, xrow], xkv_s.at[j - 1], xkv_r.at[j - 1], xpeer(j))
            for j in hop]
    start(kv_x)
    kv_own = pltpu.make_async_copy(kvsend.at[x], kv.at[:, :, 0, y, xrow], loc_sem.at[0])
    kv_own.start()
    q_x = {j: [send(q_ref.at[:, group_cols(j)], qb.at[token_rows(0)], xq_s.at[j - 1], xq_r.at[j - 1], xpeer(j)),
               send(g_ref.at[:, group_cols(j)], gb.at[token_rows(0)], xg_s.at[j - 1], xg_r.at[j - 1], xpeer(j))]
           for j in hop}
    for j in hop:
        start(q_x[j])
    q_own = [pltpu.make_async_copy(q_ref.at[:, group_cols(0)], qb.at[token_rows(0)], loc_sem.at[1]),
             pltpu.make_async_copy(g_ref.at[:, group_cols(0)], gb.at[token_rows(0)], loc_sem.at[2])]
    start(q_own)

    share = {0: [send(q_ref.at[:, group_cols(0)], qb.at[token_rows(0)], sib_s.at[0, 0], sib_r.at[0, 0], sib),
                 send(g_ref.at[:, group_cols(0)], gb.at[token_rows(0)], sib_s.at[1, 0], sib_r.at[1, 0], sib)]}
    for j in hop:
        share[j] = [send(qb.at[token_rows(j)], qb.at[token_rows(j)], sib_s.at[0, j], sib_r.at[0, j], sib),
                    send(gb.at[token_rows(j)], gb.at[token_rows(j)], sib_s.at[1, j], sib_r.at[1, j], sib)]
    start(share[0])

    stats[...] = jnp.zeros_like(stats)
    for h in range(heads):
        stats[h, 0:1] = jnp.full((1, nq), -1e30, F32)
    dq_acc[...] = jnp.zeros_like(dq_acc)

    def ring(kind, s):
        def cut(slot, a):
            if kind == 0:
                return kv.at[1:heads, a, slot, y]
            return kv.at[0, a, slot]
        a_src, b_src, by = ((0, 0, 1), (2, 3, 1), (4, 5, 1), (4, 5, 2))[s - 1]
        if s < half:
            ways = ((a_src, 2 * s, slice(None)), (b_src, 2 * s + 1, slice(None)))
        else:
            ways = ((a_src, 1, 0), (b_src, 1, 1))
        return [send(cut(src, a), cut(dst, a), ring_s.at[kind, w, s - 1], ring_r.at[kind, w, s - 1], along(way))
                for w, ((src, dst, a), way) in enumerate(zip(ways, (by, -by)))]

    def over_y(slot):
        return send(kv.at[1:heads, :, slot, y], kv.at[1:heads, :, slot, y], y_s.at[slot], y_r.at[slot], ypeer)

    def handle(s):
        for kind in range(2):
            onward = [ring(kind, n) for n in ((2,), (3, 4), (), ())[s - 1]]
            for w, copy in enumerate(ring(kind, s)):
                copy.wait_recv()
                start([copies[w] for copies in onward])
                if kind == 0 and s < half:
                    over_y(2 * s + w).start()
            if kind == 0 and s == half:
                over_y(1).start()

    kv_own.wait()
    received(kv_x)
    start(ring(0, 1))
    y_first = send(kv.at[0, :, 0, y], kv.at[0, :, 0, y], y_s.at[nz], y_r.at[nz], ypeer)
    start([y_first, over_y(0)])
    received([y_first])
    start(ring(1, 1))
    for copy in q_own:
        copy.wait()
    handle(1)
    for j in hop:
        received(q_x[j])
        start(share[j])
    handle(2)

    def pass1(s, qh, h):
        lanes = pl.ds(pl.multiple_of(h * HEAD_DIM, HEAD_DIM), HEAD_DIM)
        keys = kv[h, 0, pl.ds(2 * s, 2)].reshape(nk, HEAD_DIM)
        vals = kv[h, 1, pl.ds(2 * s, 2)].reshape(nk, HEAD_DIM)
        for t in range(hq // tq):
            ts = pl.ds(pl.multiple_of(qh * hq + t * tq, tq), tq)
            sc = dot_nt(keys, qb[ts, lanes]) * (SCALE * LOG2E)
            dp = dot_nt(vals, gb[ts, lanes])
            m_old = stats[h, 0:1, ts]
            m_new = jnp.maximum(m_old, jnp.max(sc, axis=0, keepdims=True))
            e = jnp.exp2(sc - m_new)
            a = jnp.exp2(m_old - m_new)
            e_buf[s, h, :, ts] = e
            dp_buf[s, h, :, ts] = dp
            m_buf[s, h, 0:1, ts] = m_new
            stats[h, 0:1, ts] = m_new
            stats[h, 1:2, ts] = stats[h, 1:2, ts] * a + jnp.sum(e, axis=0, keepdims=True)
            stats[h, 2:3, ts] = stats[h, 2:3, ts] * a + jnp.sum(e * dp, axis=0, keepdims=True)

    def gather_step(i, carry):
        n = i // 2
        s = n + 1
        later = lax.rem(i, 2)
        for m in range(half - 1):
            @pl.when(i == 2 * m)
            def _():
                if m >= 1:
                    handle(m + 2)
                received([over_y(2 * m + 2), over_y(2 * m + 3)])

        @pl.when(i == 1)
        def _():
            for j in [0] + hop:
                received(share[j])

        def head(h, inner):
            pass1(s, lax.rem(c + later, 2), h)
            return inner
        lax.fori_loop(0, heads, head, 0)
        return carry

    lax.fori_loop(0, 2 * (half - 1), gather_step, 0)
    def join(h):
        return send(stats.at[h], stats_in.at[h], join_s.at[h], join_r.at[h], sib)

    def last_head(h, carry):
        @pl.when(h == 1)
        def _():
            received([over_y(0), over_y(1)])

        def both(qh, inner):
            pass1(0, qh, h)
            return inner
        lax.fori_loop(0, 2, both, 0)
        join(h).start()
        return carry

    lax.fori_loop(0, heads, last_head, 0)

    def finish_stats(h):
        join(h).wait_recv()
        m1, m2 = stats[h, 0:1], stats_in[h, 0:1]
        m = jnp.maximum(m1, m2)
        a1, a2 = jnp.exp2(m1 - m), jnp.exp2(m2 - m)
        inv = 1.0 / (stats[h, 1:2] * a1 + stats_in[h, 1:2] * a2)
        fin[h, 0:1] = m
        fin[h, 1:2] = inv
        fin[h, 2:3] = (stats[h, 2:3] * a1 + stats_in[h, 2:3] * a2) * inv

    def pass2(s, h):
        lanes = pl.ds(pl.multiple_of(h * HEAD_DIM, HEAD_DIM), HEAD_DIM)
        keys = kv[h, 0, pl.ds(2 * s, 2)].reshape(nk, HEAD_DIM)
        dk = jnp.zeros((nk, HEAD_DIM), F32)
        dv = jnp.zeros((nk, HEAD_DIM), F32)
        for t in range(nq // tq):
            ts = slice(t * tq, (t + 1) * tq)
            r = jnp.exp2(m_buf[s, h, 0:1, ts] - fin[h, 0:1, ts]) * fin[h, 1:2, ts]
            p = e_buf[s, h, :, ts] * r
            ds = (p * (dp_buf[s, h, :, ts] - fin[h, 2:3, ts])).astype(BF16)
            dv = dv + dot_nn(p.astype(BF16), gb[ts, lanes])
            dk = dk + dot_nn(ds, qb[ts, lanes])
            dq_acc[h, :, ts] = dq_acc[h, :, ts] + dot_tn(keys, ds)
        part[h, 0, pl.ds(2 * s, 2)] = dk.astype(BF16).reshape(2, 2, nx * rows, HEAD_DIM)
        part[h, 1, pl.ds(2 * s, 2)] = dv.astype(BF16).reshape(2, 2, nx * rows, HEAD_DIM)

    def mine(kind, slot, a):
        return part.at[1:heads, a, slot, y] if kind == 0 else part.at[0, a, slot]

    def box(kind, w, n, a):
        return rs_buf.at[w, n, :, a] if kind == 0 else rr_buf.at[w, n, a]

    def reduce(kind, n):
        ways = []
        for w, sign in enumerate((1, -1)):
            if n == half:
                slot, a, by = 1, w, 2
            else:
                slot, a, by = 2 * n + 1 - w, slice(None), 1
            ways.append(send(mine(kind, slot, a), box(kind, w, n - 1, a),
                             red_s.at[kind, w, n - 1], red_r.at[kind, w, n - 1], along(sign * by)))
        return ways

    def reduce_y(slot):
        return send(part.at[1:heads, :, slot, 1 - y], ys_buf.at[slot], yr_s.at[slot], yr_r.at[slot], ypeer)

    def add_y(slot):
        reduce_y(slot).wait_recv()
        part[1:heads, :, slot, y] = (part[1:heads, :, slot, y].astype(F32) + ys_buf[slot].astype(F32)).astype(BF16)

    def relay(kind, n):
        for w in range(2):
            slot = 2 * n + 1 - w
            if kind == 0:
                add_y(slot)
            received([reduce(kind, n + 1)[w]] + ([reduce(kind, 4)[w]] if n == 2 else []))
            for a in range(2):
                far = n == 2 and a == w
                if kind == 0:
                    total = part[1:heads, a, slot, y].astype(F32) + rs_buf[w, n, :, a].astype(F32)
                    if far:
                        total = total + rs_buf[w, 3, :, a].astype(F32)
                    part[1:heads, a, slot, y] = total.astype(BF16)
                else:
                    total = part[0, a, slot].astype(F32) + rr_buf[w, n, a].astype(F32)
                    if far:
                        total = total + rr_buf[w, 3, a].astype(F32)
                    part[0, a, slot] = total.astype(BF16)
            reduce(kind, n)[w].start()

    order = [4, 3, 2, 1]

    def produce(t):
        s = lax.rem(half - t, half)

        def head(n, carry):
            h = lax.rem(n + 1, heads)

            @pl.when(t == 0)
            def _():
                finish_stats(h)
            pass2(s, h)

            @pl.when(n == heads - 2)
            def _():
                for k, place in enumerate(order):
                    @pl.when(t == k)
                    def _():
                        start([reduce_y(slot) for slot in ((2 * place + 1, 2 * place) if place < half else (1,))])
            return carry
        lax.fori_loop(0, heads, head, 0)
        for k, place in enumerate(order):
            if place > 2:
                @pl.when(t == k)
                def _():
                    start(reduce(1, place))

    def pass_on(t):
        for k, place in enumerate(order):
            @pl.when(t == k)
            def _():
                if place < 3:
                    relay(1, place)
                    relay(0, place)
                elif place == 3:
                    for w in range(2):
                        add_y(7 - w)
                        reduce(0, 3)[w].start()
                else:
                    add_y(1)
                    start(reduce(0, 4))

    dq_sib = send(dqb.at[1 - c], dqr, sib_s.at[0, nx], sib_r.at[0, nx], sib)

    def reduce_step(t, carry):
        @pl.when(t < half)
        def _():
            produce(t)

        @pl.when(t == half)
        def _():
            start([reduce_y(0)])
            for h in range(heads):
                for cc in range(2):
                    for xs in range(nx):
                        at = (cc * nx + xs) * tok
                        dqb[cc, xs, :, h * HEAD_DIM:(h + 1) * HEAD_DIM] = (
                            jnp.transpose(dq_acc[h, :, at:at + tok]) * SCALE).astype(BF16)
            dq_sib.start()

        @pl.when(t > 0)
        def _():
            pass_on(t - 1)
        return carry

    lax.fori_loop(0, half + 1, reduce_step, 0)

    dq_sib.wait()
    for xs in range(nx):
        dqs[xs] = (dqb[c, xs].astype(F32) + dqr[xs].astype(F32)).astype(BF16)
    dq_x = [send(dqs.at[(x + j) % nx], dq_out.at[:, group_cols(0)], xd_s.at[j - 1], xd_r.at[j - 1], xpeer(j))
            for j in hop]
    start(dq_x)
    dq_own = pltpu.make_async_copy(dqs.at[x], dq_out.at[:, group_cols(0)], loc_sem.at[3])
    dq_own.start()

    received(reduce(1, 1))

    def total_r(a):
        total = part[0, a, 0].astype(F32)
        for w in range(2):
            total = total + rr_buf[w, 0, a].astype(F32)
        return total

    def total_s(h, a):
        total = part[h, a, 0, y].astype(F32) + ys_buf[0, h - 1, a].astype(F32)
        for w in range(2):
            total = total + rs_buf[w, 0, h - 1, a].astype(F32)
        return total

    for a in range(2):
        total = total_r(a) * SCALE if a == 0 else total_r(a)
        total = total.astype(BF16)
        for ys in range(2):
            for xs in range(nx):
                zero_send[xs, ys, a] = total[ys, xs * rows:(xs + 1) * rows]
    zero_x = [send(zero_send.at[(x + j) % nx, y], zero.at[x, y], xo_s.at[1, j], xo_r.at[1, j], xpeer(j)) for j in hop]
    zero_x += [send(zero_send.at[(x + j) % nx, 1 - y], zero.at[x, y], xo_s.at[2, j], xo_r.at[2, j], crossed(j))
               for j in hop + [0]]
    start(zero_x)
    zero_own = pltpu.make_async_copy(zero_send.at[x, y], zero.at[x, y], loc_sem.at[5])
    zero_own.start()

    reduce_y(0).wait_recv()
    received(reduce(0, 1))
    for h in range(1, heads):
        for a in range(2):
            total = total_s(h, a) * SCALE if a == 0 else total_s(h, a)
            total = total.astype(BF16)
            for xs in range(nx):
                gkv_send[xs, h, a] = total[xs * rows:(xs + 1) * rows]
    out_x = [send(gkv_send.at[(x + j) % nx, 1:heads], gkv.at[x, 1:heads], xo_s.at[0, j], xo_r.at[0, j], xpeer(j))
             for j in hop]
    start(out_x)
    out_own = pltpu.make_async_copy(gkv_send.at[x, 1:heads], gkv.at[x, 1:heads], loc_sem.at[4])
    out_own.start()
    zero_own.wait()
    received(zero_x)
    for g in range(nx):
        for a in range(2):
            gkv[g, 0, a] = (zero[g, 0, a].astype(F32) + zero[g, 1, a].astype(F32)).astype(BF16)

    sent(kv_x)
    for j in hop:
        sent(q_x[j])
    for j in [0] + hop:
        sent(share[j])
    for kind in range(2):
        for s in range(1, half + 1):
            sent(ring(kind, s) + reduce(kind, s))
    for slot in range(nz):
        sent([over_y(slot), reduce_y(slot)])
    sent([y_first])
    sent(zero_x)
    for h in range(heads):
        join(h).wait_send()
    dq_own.wait()
    for copy in dq_x:
        copy.wait()
    out_own.wait()
    for copy in out_x:
        copy.wait()


def place(nx, heads, tok, rows, idx_ref, dq_ref, gkv_ref, dq_out, dk_out, dv_out):
    dq_out[...] = dq_ref[...]
    hot = one_hot(idx_ref, tok, rows)
    for a, ref in enumerate((dk_out, dv_out)):
        for g in range(nx):
            for h in range(heads):
                col = (g * heads + h) * HEAD_DIM
                ref[:, col:col + HEAD_DIM] = dot_nn(hot, gkv_ref[g, h, a]).astype(BF16)


def per_device(nx, nz, queries, key_input, value_input, grad_out, keep_index):
    tok, columns = queries.shape
    rows = keep_index.shape[0]
    heads = columns // HEAD_DIM // nx
    width = heads * HEAD_DIM
    half = nz // 2
    nq = 2 * nx * tok
    nk = 4 * nx * rows
    slab = (nx * rows, HEAD_DIM)
    dma = pltpu.SemaphoreType.DMA
    vmem = pltpu.VMEM
    out = jax.ShapeDtypeStruct((tok, columns), BF16)
    compact = (nx, heads, 2, rows, HEAD_DIM)
    in_vmem = pl.BlockSpec(memory_space=pltpu.VMEM)
    in_any = pl.BlockSpec(memory_space=pl.ANY)
    flops = 2 * 6 * heads * nq * (half * nk) * HEAD_DIM
    index = keep_index.reshape(1, rows)
    dq, gkv = pl.pallas_call(
        functools.partial(kernel, nx, nz, heads, tok, rows),
        out_shape=(out, jax.ShapeDtypeStruct(compact, BF16)),
        in_specs=[in_vmem, in_vmem, in_vmem, in_any, in_any],
        out_specs=(in_vmem, in_vmem),
        scratch_shapes=[
            vmem(compact, BF16),
            vmem((heads, 2, nz, 2) + slab, BF16),
            vmem((nq, width), BF16),
            vmem((nq, width), BF16),
            vmem((half, heads, nk, nq), F32),
            vmem((half, heads, nk, nq), F32),
            vmem((half, heads, 8, nq), F32),
            vmem((heads, 8, nq), F32),
            vmem((heads, 8, nq), F32),
            vmem((heads, 8, nq), F32),
            vmem((heads, HEAD_DIM, nq), F32),
            vmem((2, nx, tok, width), BF16),
            vmem((nx, tok, width), BF16),
            vmem((nx, tok, width), BF16),
            vmem((heads, 2, nz, 2) + slab, BF16),
            vmem((2, half, heads - 1, 2) + slab, BF16),
            vmem((2, half, 2, 2) + slab, BF16),
            vmem((nz, heads - 1, 2) + slab, BF16),
            vmem(compact, BF16),
            vmem((nx, 2, 2, rows, HEAD_DIM), BF16),
            vmem((nx, 2, 2, rows, HEAD_DIM), BF16),
            dma((6,)),
            dma((nx - 1,)), dma((nx - 1,)),
            dma((nx - 1,)), dma((nx - 1,)),
            dma((nx - 1,)), dma((nx - 1,)),
            dma((nz + 1,)), dma((nz + 1,)),
            dma((2, 2, half)), dma((2, 2, half)),
            dma((2, nx + 1)), dma((2, nx + 1)),
            dma((heads,)), dma((heads,)),
            dma((2, 2, half)), dma((2, 2, half)),
            dma((nz + 1,)), dma((nz + 1,)),
            dma((3, nx)), dma((3, nx)),
            dma((nx - 1,)), dma((nx - 1,)),
        ],
        compiler_params=pltpu.CompilerParams(
            collective_id=0, has_side_effects=True, vmem_limit_bytes=56 * 2 ** 20),
        cost_estimate=pl.CostEstimate(
            flops=flops, bytes_accessed=7 * tok * columns * 2, transcendentals=heads * nq * half * nk),
    )(index, key_input, value_input, queries, grad_out)
    return pl.pallas_call(
        functools.partial(place, nx, heads, tok, rows),
        out_shape=(out, out, out),
        in_specs=[in_vmem] * 3,
        out_specs=(in_vmem,) * 3,
    )(index, dq, gkv)


def build(mesh, nx, nz):
    rows_spec = P(("rep", "blk", "uly"), None)
    return jax.shard_map(
        functools.partial(per_device, nx, nz), mesh=mesh,
        in_specs=(rows_spec,) * 4 + (P(("rep", "blk", "uly")),),
        out_specs=(rows_spec,) * 3, check_vma=False)


def solution(mesh):
    return build(mesh, 4, 8)
```

```python
import functools

import jax
import jax.numpy as jnp
from jax import lax
from jax.experimental import pallas as pl
from jax.experimental.pallas import tpu as pltpu
from jax.sharding import PartitionSpec as P

HEAD_DIM = 128
CELL = 8
SCALE = HEAD_DIM ** -0.5
LOG2E = 1.4426950408889634
F32 = jnp.float32
BF16 = jnp.bfloat16
ULY = 4


def dot_nn(a, b):
    return lax.dot_general(a, b, (((1,), (0,)), ((), ())), preferred_element_type=F32)


def dot_nt(a, b):
    return lax.dot_general(a, b, (((1,), (1,)), ((), ())), preferred_element_type=F32)


def dot_tn(a, b):
    return lax.dot_general(a, b, (((0,), (0,)), ((), ())), preferred_element_type=F32)


def one_hot(idx_ref, tok, rows):
    return (lax.broadcasted_iota(jnp.int32, (tok, rows), 0)
            == lax.rem(idx_ref[...], tok)).astype(F32).astype(BF16)


def kernel(
    nx, nz, heads, tok, rows,
    idx_ref, k_ref, v_ref, q_ref, g_ref,
    dq_out, gkv,
    kvsend, kv, qb, gb, e_buf, dp_buf, m_buf, stats, stats_in, fin,
    dq_acc, dqb, dqr, dqs, part, rs_buf, rr_buf, ys_buf, gkv_send, zero_send, zero,
    loc_sem, xkv_s, xkv_r, xq_s, xq_r, xg_s, xg_r, y_s, y_r,
    ring_s, ring_r, sib_s, sib_r, join_s, join_r, red_s, red_r, yr_s, yr_r, xo_s, xo_r, xd_s, xd_r,
):
    width = heads * HEAD_DIM
    half = nz // 2
    hq = nx * tok
    nq = 2 * hq
    nk = 4 * nx * rows
    tq = min(512, hq)
    blk = lax.axis_index("blk")
    uly = lax.axis_index("uly")
    x = blk // nz
    z = blk % nz
    y = uly // 2
    c = uly % 2

    def along(by):
        return {"blk": x * nz + (z + nz + by) % nz}

    ypeer = {"uly": (1 - y) * 2 + c}
    sib = {"uly": y * 2 + (1 - c)}
    hop = [1, nx - 1] + list(range(2, nx - 1)) if nx > 2 else [1]

    def xpeer(j):
        return {"blk": ((x + j) % nx) * nz + z}

    def crossed(j):
        return {"blk": ((x + j) % nx) * nz + z, "uly": (1 - y) * 2 + c}

    def send(src, dst, s_sem, r_sem, dev):
        return pltpu.make_async_remote_copy(
            src_ref=src, dst_ref=dst, send_sem=s_sem, recv_sem=r_sem,
            device_id=dev, device_id_type=pl.DeviceIdType.MESH)

    def start(copies):
        for copy in copies:
            copy.start()

    def received(copies):
        for copy in copies:
            copy.wait_recv()

    def sent(copies):
        for copy in copies:
            copy.wait_send()

    barrier = pltpu.get_barrier_semaphore()
    others = [xpeer(j) for j in hop] + [crossed(j) for j in hop] + [along(1), along(-1), along(2), along(-2), ypeer, sib]
    for dev in others:
        pl.semaphore_signal(barrier, inc=1, device_id=dev, device_id_type=pl.DeviceIdType.MESH)

    hot = one_hot(idx_ref, tok, rows)
    for a, ref in enumerate((k_ref, v_ref)):
        for g in range(nx):
            for h in range(heads):
                col = (g * heads + h) * HEAD_DIM
                kvsend[g, h, a] = dot_tn(hot, ref[:, col:col + HEAD_DIM]).astype(BF16)

    pl.semaphore_wait(barrier, len(others))

    xrow = pl.ds(pl.multiple_of(x * rows, rows), rows)

    def token_rows(j):
        return pl.ds(pl.multiple_of((c * nx + (x + nx - j) % nx) * tok, tok), tok)

    def group_cols(j):
        return pl.ds(pl.multiple_of(((x + j) % nx) * width, width), width)

    kv_x = [send(kvsend.at[(x + j) % nx], kv.at[:, :, 0, y, xrow], xkv_s.at[j - 1], xkv_r.at[j - 1], xpeer(j))
            for j in hop]
    start(kv_x)
    kv_own = pltpu.make_async_copy(kvsend.at[x], kv.at[:, :, 0, y, xrow], loc_sem.at[0])
    kv_own.start()
    q_x = {j: [send(q_ref.at[:, group_cols(j)], qb.at[token_rows(0)], xq_s.at[j - 1], xq_r.at[j - 1], xpeer(j)),
               send(g_ref.at[:, group_cols(j)], gb.at[token_rows(0)], xg_s.at[j - 1], xg_r.at[j - 1], xpeer(j))]
           for j in hop}
    for j in hop:
        start(q_x[j])
    q_own = [pltpu.make_async_copy(q_ref.at[:, group_cols(0)], qb.at[token_rows(0)], loc_sem.at[1]),
             pltpu.make_async_copy(g_ref.at[:, group_cols(0)], gb.at[token_rows(0)], loc_sem.at[2])]
    start(q_own)

    share = {0: [send(q_ref.at[:, group_cols(0)], qb.at[token_rows(0)], sib_s.at[0, 0], sib_r.at[0, 0], sib),
                 send(g_ref.at[:, group_cols(0)], gb.at[token_rows(0)], sib_s.at[1, 0], sib_r.at[1, 0], sib)]}
    for j in hop:
        share[j] = [send(qb.at[token_rows(j)], qb.at[token_rows(j)], sib_s.at[0, j], sib_r.at[0, j], sib),
                    send(gb.at[token_rows(j)], gb.at[token_rows(j)], sib_s.at[1, j], sib_r.at[1, j], sib)]
    start(share[0])

    stats[...] = jnp.zeros_like(stats)
    for h in range(heads):
        stats[h, 0:1] = jnp.full((1, nq), -1e30, F32)
    dq_acc[...] = jnp.zeros_like(dq_acc)

    def ring(kind, s):
        def cut(slot, a):
            if kind == 0:
                return kv.at[1:heads, a, slot, y]
            return kv.at[0, a, slot]
        a_src, b_src, by = ((0, 0, 1), (2, 3, 1), (4, 5, 1), (4, 5, 2))[s - 1]
        if s < half:
            ways = ((a_src, 2 * s, slice(None)), (b_src, 2 * s + 1, slice(None)))
        else:
            ways = ((a_src, 1, 0), (b_src, 1, 1))
        return [send(cut(src, a), cut(dst, a), ring_s.at[kind, w, s - 1], ring_r.at[kind, w, s - 1], along(way))
                for w, ((src, dst, a), way) in enumerate(zip(ways, (by, -by)))]

    def over_y(slot):
        return send(kv.at[1:heads, :, slot, y], kv.at[1:heads, :, slot, y], y_s.at[slot], y_r.at[slot], ypeer)

    def handle(s):
        for kind in range(2):
            onward = [ring(kind, n) for n in ((2,), (3, 4), (), ())[s - 1]]
            for w, copy in enumerate(ring(kind, s)):
                copy.wait_recv()
                start([copies[w] for copies in onward])
                if kind == 0 and s < half:
                    over_y(2 * s + w).start()
            if kind == 0 and s == half:
                over_y(1).start()

    kv_own.wait()
    received(kv_x)
    start(ring(0, 1))
    y_first = send(kv.at[0, :, 0, y], kv.at[0, :, 0, y], y_s.at[nz], y_r.at[nz], ypeer)
    start([y_first, over_y(0)])
    received([y_first])
    start(ring(1, 1))
    for copy in q_own:
        copy.wait()
    handle(1)
    for j in hop:
        received(q_x[j])
        start(share[j])
    handle(2)

    def pass1(s, qh, h):
        lanes = pl.ds(pl.multiple_of(h * HEAD_DIM, HEAD_DIM), HEAD_DIM)
        keys = kv[h, 0, pl.ds(2 * s, 2)].reshape(nk, HEAD_DIM)
        vals = kv[h, 1, pl.ds(2 * s, 2)].reshape(nk, HEAD_DIM)
        for t in range(hq // tq):
            ts = pl.ds(pl.multiple_of(qh * hq + t * tq, tq), tq)
            sc = dot_nt(keys, qb[ts, lanes]) * (SCALE * LOG2E)
            dp = dot_nt(vals, gb[ts, lanes])
            m_old = stats[h, 0:1, ts]
            m_new = jnp.maximum(m_old, jnp.max(sc, axis=0, keepdims=True))
            e = jnp.exp2(sc - m_new)
            a = jnp.exp2(m_old - m_new)
            e_buf[s, h, :, ts] = e
            dp_buf[s, h, :, ts] = dp
            m_buf[s, h, 0:1, ts] = m_new
            stats[h, 0:1, ts] = m_new
            stats[h, 1:2, ts] = stats[h, 1:2, ts] * a + jnp.sum(e, axis=0, keepdims=True)
            stats[h, 2:3, ts] = stats[h, 2:3, ts] * a + jnp.sum(e * dp, axis=0, keepdims=True)

    def gather_step(i, carry):
        n = i // 2
        s = n + 1
        later = lax.rem(i, 2)
        for m in range(half - 1):
            @pl.when(i == 2 * m)
            def _():
                if m == 1:
                    handle(3)
                received([over_y(2 * m + 2), over_y(2 * m + 3)])

        @pl.when(i == 1)
        def _():
            for j in [0] + hop:
                received(share[j])

        @pl.when(i == 3)
        def _():
            handle(4)

        def head(h, inner):
            pass1(s, lax.rem(c + later, 2), h)
            return inner
        lax.fori_loop(0, heads, head, 0)
        return carry

    lax.fori_loop(0, 2 * (half - 1), gather_step, 0)
    def join(h):
        return send(stats.at[h], stats_in.at[h], join_s.at[h], join_r.at[h], sib)

    def last_head(h, carry):
        @pl.when(h == 1)
        def _():
            received([over_y(0), over_y(1)])

        def both(qh, inner):
            pass1(0, qh, h)
            return inner
        lax.fori_loop(0, 2, both, 0)
        join(h).start()
        return carry

    lax.fori_loop(0, heads, last_head, 0)

    def finish_stats(h):
        join(h).wait_recv()
        m1, m2 = stats[h, 0:1], stats_in[h, 0:1]
        m = jnp.maximum(m1, m2)
        a1, a2 = jnp.exp2(m1 - m), jnp.exp2(m2 - m)
        inv = 1.0 / (stats[h, 1:2] * a1 + stats_in[h, 1:2] * a2)
        fin[h, 0:1] = m
        fin[h, 1:2] = inv
        fin[h, 2:3] = (stats[h, 2:3] * a1 + stats_in[h, 2:3] * a2) * inv

    def pass2(s, h):
        lanes = pl.ds(pl.multiple_of(h * HEAD_DIM, HEAD_DIM), HEAD_DIM)
        keys = kv[h, 0, pl.ds(2 * s, 2)].reshape(nk, HEAD_DIM)
        dk = jnp.zeros((nk, HEAD_DIM), F32)
        dv = jnp.zeros((nk, HEAD_DIM), F32)
        for t in range(nq // tq):
            ts = slice(t * tq, (t + 1) * tq)
            r = jnp.exp2(m_buf[s, h, 0:1, ts] - fin[h, 0:1, ts]) * fin[h, 1:2, ts]
            p = e_buf[s, h, :, ts] * r
            ds = (p * (dp_buf[s, h, :, ts] - fin[h, 2:3, ts])).astype(BF16)
            dv = dv + dot_nn(p.astype(BF16), gb[ts, lanes])
            dk = dk + dot_nn(ds, qb[ts, lanes])
            dq_acc[h, :, ts] = dq_acc[h, :, ts] + dot_tn(keys, ds)
        part[h, 0, pl.ds(2 * s, 2)] = dk.astype(BF16).reshape(2, 2, nx * rows, HEAD_DIM)
        part[h, 1, pl.ds(2 * s, 2)] = dv.astype(BF16).reshape(2, 2, nx * rows, HEAD_DIM)

    def mine(kind, slot, a):
        return part.at[1:heads, a, slot, y] if kind == 0 else part.at[0, a, slot]

    def box(kind, w, n, a):
        return rs_buf.at[w, n, :, a] if kind == 0 else rr_buf.at[w, n, a]

    def reduce(kind, n):
        ways = []
        for w, sign in enumerate((1, -1)):
            if n == half:
                slot, a, by = 1, w, 2
            else:
                slot, a, by = 2 * n + 1 - w, slice(None), 1
            ways.append(send(mine(kind, slot, a), box(kind, w, n - 1, a),
                             red_s.at[kind, w, n - 1], red_r.at[kind, w, n - 1], along(sign * by)))
        return ways

    def reduce_y(slot):
        return send(part.at[1:heads, :, slot, 1 - y], ys_buf.at[slot], yr_s.at[slot], yr_r.at[slot], ypeer)

    def add_y(slot):
        reduce_y(slot).wait_recv()
        part[1:heads, :, slot, y] = (part[1:heads, :, slot, y].astype(F32) + ys_buf[slot].astype(F32)).astype(BF16)

    def relay(kind, n):
        for w in range(2):
            slot = 2 * n + 1 - w
            if kind == 0:
                add_y(slot)
            received([reduce(kind, n + 1)[w]] + ([reduce(kind, 4)[w]] if n == 2 else []))
            for a in range(2):
                far = n == 2 and a == w
                if kind == 0:
                    total = part[1:heads, a, slot, y].astype(F32) + rs_buf[w, n, :, a].astype(F32)
                    if far:
                        total = total + rs_buf[w, 3, :, a].astype(F32)
                    part[1:heads, a, slot, y] = total.astype(BF16)
                else:
                    total = part[0, a, slot].astype(F32) + rr_buf[w, n, a].astype(F32)
                    if far:
                        total = total + rr_buf[w, 3, a].astype(F32)
                    part[0, a, slot] = total.astype(BF16)
            reduce(kind, n)[w].start()

    order = [4, 3, 2, 1]

    def produce(t):
        s = lax.rem(half - t, half)

        def head(n, carry):
            h = lax.rem(n + 1, heads)

            @pl.when(t == 0)
            def _():
                finish_stats(h)
            pass2(s, h)

            @pl.when(n == heads - 2)
            def _():
                for k, place in enumerate(order):
                    @pl.when(t == k)
                    def _():
                        start([reduce_y(slot) for slot in ((2 * place + 1, 2 * place) if place < half else (1,))])
            return carry
        lax.fori_loop(0, heads, head, 0)
        for k, place in enumerate(order):
            if place > 2:
                @pl.when(t == k)
                def _():
                    start(reduce(1, place))

    def pass_on(t):
        for k, place in enumerate(order):
            @pl.when(t == k)
            def _():
                if place < 3:
                    relay(1, place)
                    relay(0, place)
                elif place == 3:
                    for w in range(2):
                        add_y(7 - w)
                        reduce(0, 3)[w].start()
                else:
                    add_y(1)
                    start(reduce(0, 4))

    dq_sib = send(dqb.at[1 - c], dqr, sib_s.at[0, nx], sib_r.at[0, nx], sib)

    def reduce_step(t, carry):
        @pl.when(t < half)
        def _():
            produce(t)

        @pl.when(t == half)
        def _():
            start([reduce_y(0)])
            for h in range(heads):
                for cc in range(2):
                    for xs in range(nx):
                        at = (cc * nx + xs) * tok
                        dqb[cc, xs, :, h * HEAD_DIM:(h + 1) * HEAD_DIM] = (
                            jnp.transpose(dq_acc[h, :, at:at + tok]) * SCALE).astype(BF16)
            dq_sib.start()

        @pl.when(t > 0)
        def _():
            pass_on(t - 1)
        return carry

    lax.fori_loop(0, half + 1, reduce_step, 0)

    dq_sib.wait()
    for xs in range(nx):
        dqs[xs] = (dqb[c, xs].astype(F32) + dqr[xs].astype(F32)).astype(BF16)
    dq_x = [send(dqs.at[(x + j) % nx], dq_out.at[:, group_cols(0)], xd_s.at[j - 1], xd_r.at[j - 1], xpeer(j))
            for j in hop]
    start(dq_x)
    dq_own = pltpu.make_async_copy(dqs.at[x], dq_out.at[:, group_cols(0)], loc_sem.at[3])
    dq_own.start()

    received(reduce(1, 1))

    def total_r(a):
        total = part[0, a, 0].astype(F32)
        for w in range(2):
            total = total + rr_buf[w, 0, a].astype(F32)
        return total

    def total_s(h, a):
        total = part[h, a, 0, y].astype(F32) + ys_buf[0, h - 1, a].astype(F32)
        for w in range(2):
            total = total + rs_buf[w, 0, h - 1, a].astype(F32)
        return total

    for a in range(2):
        total = total_r(a) * SCALE if a == 0 else total_r(a)
        total = total.astype(BF16)
        for ys in range(2):
            for xs in range(nx):
                zero_send[xs, ys, a] = total[ys, xs * rows:(xs + 1) * rows]
    zero_x = [send(zero_send.at[(x + j) % nx, y], zero.at[x, y], xo_s.at[1, j], xo_r.at[1, j], xpeer(j)) for j in hop]
    zero_x += [send(zero_send.at[(x + j) % nx, 1 - y], zero.at[x, y], xo_s.at[2, j], xo_r.at[2, j], crossed(j))
               for j in hop + [0]]
    start(zero_x)
    zero_own = pltpu.make_async_copy(zero_send.at[x, y], zero.at[x, y], loc_sem.at[5])
    zero_own.start()

    reduce_y(0).wait_recv()
    received(reduce(0, 1))
    for h in range(1, heads):
        for a in range(2):
            total = total_s(h, a) * SCALE if a == 0 else total_s(h, a)
            total = total.astype(BF16)
            for xs in range(nx):
                gkv_send[xs, h, a] = total[xs * rows:(xs + 1) * rows]
    out_x = [send(gkv_send.at[(x + j) % nx, 1:heads], gkv.at[x, 1:heads], xo_s.at[0, j], xo_r.at[0, j], xpeer(j))
             for j in hop]
    start(out_x)
    out_own = pltpu.make_async_copy(gkv_send.at[x, 1:heads], gkv.at[x, 1:heads], loc_sem.at[4])
    out_own.start()
    zero_own.wait()
    received(zero_x)
    for g in range(nx):
        for a in range(2):
            gkv[g, 0, a] = (zero[g, 0, a].astype(F32) + zero[g, 1, a].astype(F32)).astype(BF16)

    sent(kv_x)
    for j in hop:
        sent(q_x[j])
    for j in [0] + hop:
        sent(share[j])
    for kind in range(2):
        for s in range(1, half + 1):
            sent(ring(kind, s) + reduce(kind, s))
    for slot in range(nz):
        sent([over_y(slot), reduce_y(slot)])
    sent([y_first])
    sent(zero_x)
    for h in range(heads):
        join(h).wait_send()
    dq_own.wait()
    for copy in dq_x:
        copy.wait()
    out_own.wait()
    for copy in out_x:
        copy.wait()


def place(nx, heads, tok, rows, idx_ref, dq_ref, gkv_ref, dq_out, dk_out, dv_out):
    dq_out[...] = dq_ref[...]
    hot = one_hot(idx_ref, tok, rows)
    for a, ref in enumerate((dk_out, dv_out)):
        for g in range(nx):
            for h in range(heads):
                col = (g * heads + h) * HEAD_DIM
                ref[:, col:col + HEAD_DIM] = dot_nn(hot, gkv_ref[g, h, a]).astype(BF16)


def per_device(nx, nz, queries, key_input, value_input, grad_out, keep_index):
    tok, columns = queries.shape
    rows = keep_index.shape[0]
    heads = columns // HEAD_DIM // nx
    width = heads * HEAD_DIM
    half = nz // 2
    nq = 2 * nx * tok
    nk = 4 * nx * rows
    slab = (nx * rows, HEAD_DIM)
    dma = pltpu.SemaphoreType.DMA
    vmem = pltpu.VMEM
    out = jax.ShapeDtypeStruct((tok, columns), BF16)
    compact = (nx, heads, 2, rows, HEAD_DIM)
    in_vmem = pl.BlockSpec(memory_space=pltpu.VMEM)
    in_any = pl.BlockSpec(memory_space=pl.ANY)
    flops = 2 * 6 * heads * nq * (half * nk) * HEAD_DIM
    index = keep_index.reshape(1, rows)
    dq, gkv = pl.pallas_call(
        functools.partial(kernel, nx, nz, heads, tok, rows),
        out_shape=(out, jax.ShapeDtypeStruct(compact, BF16)),
        in_specs=[in_vmem, in_vmem, in_vmem, in_any, in_any],
        out_specs=(in_vmem, in_vmem),
        scratch_shapes=[
            vmem(compact, BF16),
            vmem((heads, 2, nz, 2) + slab, BF16),
            vmem((nq, width), BF16),
            vmem((nq, width), BF16),
            vmem((half, heads, nk, nq), F32),
            vmem((half, heads, nk, nq), F32),
            vmem((half, heads, 8, nq), F32),
            vmem((heads, 8, nq), F32),
            vmem((heads, 8, nq), F32),
            vmem((heads, 8, nq), F32),
            vmem((heads, HEAD_DIM, nq), F32),
            vmem((2, nx, tok, width), BF16),
            vmem((nx, tok, width), BF16),
            vmem((nx, tok, width), BF16),
            vmem((heads, 2, nz, 2) + slab, BF16),
            vmem((2, half, heads - 1, 2) + slab, BF16),
            vmem((2, half, 2, 2) + slab, BF16),
            vmem((nz, heads - 1, 2) + slab, BF16),
            vmem(compact, BF16),
            vmem((nx, 2, 2, rows, HEAD_DIM), BF16),
            vmem((nx, 2, 2, rows, HEAD_DIM), BF16),
            dma((6,)),
            dma((nx - 1,)), dma((nx - 1,)),
            dma((nx - 1,)), dma((nx - 1,)),
            dma((nx - 1,)), dma((nx - 1,)),
            dma((nz + 1,)), dma((nz + 1,)),
            dma((2, 2, half)), dma((2, 2, half)),
            dma((2, nx + 1)), dma((2, nx + 1)),
            dma((heads,)), dma((heads,)),
            dma((2, 2, half)), dma((2, 2, half)),
            dma((nz + 1,)), dma((nz + 1,)),
            dma((3, nx)), dma((3, nx)),
            dma((nx - 1,)), dma((nx - 1,)),
        ],
        compiler_params=pltpu.CompilerParams(
            collective_id=0, has_side_effects=True, vmem_limit_bytes=56 * 2 ** 20),
        cost_estimate=pl.CostEstimate(
            flops=flops, bytes_accessed=7 * tok * columns * 2, transcendentals=heads * nq * half * nk),
    )(index, key_input, value_input, queries, grad_out)
    return pl.pallas_call(
        functools.partial(place, nx, heads, tok, rows),
        out_shape=(out, out, out),
        in_specs=[in_vmem] * 3,
        out_specs=(in_vmem,) * 3,
    )(index, dq, gkv)


def build(mesh, nx, nz):
    rows_spec = P(("rep", "blk", "uly"), None)
    return jax.shard_map(
        functools.partial(per_device, nx, nz), mesh=mesh,
        in_specs=(rows_spec,) * 4 + (P(("rep", "blk", "uly")),),
        out_specs=(rows_spec,) * 3, check_vma=False)


def solution(mesh):
    return build(mesh, 4, 8)
```
